32 devices in a mesh: dom: 8 (over y, x, core), rep: 4 (over z).
Axes of the slice: x: 2, y: 2, z: 4, core: 2. Of those that a mesh axis runs over, the one named last changes fastest.
Arguments:
- features: bfloat16 [8192, 256], P(('dom', 'rep')), may hold values from -6 to 6
- weight: bfloat16 [256, 256], replicated, may hold values from -0.375 to 0.375
- tile_cols: int32 [64, 8], P(('dom', 'rep')), may hold values from 0 to 7
- tile_vals: bfloat16 [64, 8, 128, 128], P(('dom', 'rep')), may hold values from -0.1875 to 0.1875
- tile_counts: int32 [64], P(('dom', 'rep')), may hold values from 1 to 8
- send_rows: int32 [32, 8, 16], P(('dom', 'rep')), may hold values from 0 to 255
- bnd_adj: bfloat16 [8192, 128], P(('dom', 'rep')), may hold values from -0.5 to 0.5
- cotangent: bfloat16 [8192, 256], P(('dom', 'rep')), may hold values from -6 to 6
Outputs:
- output: bfloat16 [8192, 256], P(('dom', 'rep'))
- grad_features: bfloat16 [8192, 256], P(('dom', 'rep'))
- grad_weight: float32 [256, 256], replicated
The draws below stay inside these ranges and needn't reach their ends.
Inputs may be any that keep to these rules, and one draw needn't show every extreme that they name: `send_rows`: local row index on the sending device; rows may repeat.
All inputs are finite; a program needn't handle non-finite values.
Results may differ from the reference program's by a relative error of at most 0.0085.
Values may be sent and summed in bfloat16 or wider, within the bound.
No kernel may reach another device: no remote copies, remote signals or barrier semaphores. Data moves between devices by JAX's collectives and lax.ppermute only.
A program may use at most 64 MiB of HBM per device.

```python
import jax
import jax.numpy as jnp
from jax import lax

F = 256
H = 256
K = 8
B = 16
ROWS_DEV = 256
NODES = 8192
N_DOM = 8
N_REP = 4


def place_ends(values, stream_key, least, top_value):
    extent = values.shape
    spot = [jax.random.randint(jax.random.fold_in(stream_key, axis), (), 0, extent[axis]) for axis in range(len(extent))]
    values = values.at[tuple(spot)].set(least)
    longest = extent.index(max(extent))
    spot[longest] = (spot[longest] + 1) % extent[longest]
    return values.at[tuple(spot)].set(top_value)


def steps_of(key, dims, shards, least, largest):
    gain = 1.0
    for axis_at, shards_of in shards:
        draws = jax.random.uniform(jax.random.fold_in(jax.random.fold_in(key, 6), axis_at), (shards_of,), jnp.float32, least / len(shards), largest / len(shards))
        gain = gain * jnp.repeat(jnp.exp(draws), dims[axis_at] // shards_of).reshape((-1,) + (1,) * (len(dims) - 1 - axis_at))
    return gain


def gaussian(key, shape, scale, most, pieces=(), kind=jnp.bfloat16):
    values = jax.random.normal(key, shape, jnp.float32) * scale
    if len(pieces) > 0:
        values = steps_of(key, shape, pieces, -0.22, 0.18) * values
    return jnp.clip(values, min=-most, max=most).astype(kind)


def setup_inputs(seed: int = 0) -> dict:
    splits = jax.random.split(jax.random.key(seed), 9)
    features = gaussian(splits[0], (NODES, F), 1.0, 6.0, ((0, 32),))
    weight = gaussian(splits[1], (F, H), F ** -0.5, 0.375)
    tile_cols = place_ends(jax.random.randint(splits[2], (NODES // 128, K), 0, N_REP * ROWS_DEV // 128), jax.random.fold_in(splits[2], 1), 0, (N_REP * ROWS_DEV // 128) - 1).astype(jnp.int32)
    tile_vals = gaussian(splits[3], (NODES // 128, K, 128, 128), (K * 128) ** -0.5, 0.1875, ((0, 32),))
    tile_counts = place_ends(jax.random.randint(splits[4], (NODES // 128,), 1, K + 1), jax.random.fold_in(splits[4], 1), 1, K).astype(jnp.int32)
    send_rows = place_ends(jax.random.randint(splits[5], (N_DOM * N_REP, N_DOM, B), 0, ROWS_DEV), jax.random.fold_in(splits[5], 1), 0, ROWS_DEV - 1).astype(jnp.int32)
    bnd_adj = gaussian(splits[6], (NODES, N_DOM * B), (N_DOM * B) ** -0.5, 0.5, ((0, 32),))
    cotangent = gaussian(splits[7], (NODES, H), 1.0, 6.0, ((0, 32),))
    return dict(features=features, weight=weight, tile_cols=tile_cols, tile_vals=tile_vals, tile_counts=tile_counts, send_rows=send_rows, bnd_adj=bnd_adj, cotangent=cotangent)


def reference(features, weight, tile_cols, tile_vals, tile_counts, send_rows, bnd_adj, cotangent):
    row_tiles = ROWS_DEV // 128
    group_tiles = N_REP * row_tiles
    projected = jnp.dot(features, weight, preferred_element_type=jnp.float32).astype(jnp.bfloat16)
    live = jnp.arange(K)[None, :] < tile_counts[:, None]
    masked = jnp.where(live[:, :, None, None], tile_vals, jnp.zeros_like(tile_vals))
    cols = tile_cols.reshape(N_DOM, group_tiles, K)
    vals = masked.reshape(N_DOM, group_tiles, K, 128, 128)
    panels = projected.reshape(N_DOM, group_tiles, 128, H)

    def forward_group(items):
        panel, col, val = items
        chosen = panel[col]
        return jnp.einsum("tkij,tkjh->tih", val.astype(jnp.float32), chosen.astype(jnp.float32))

    local = lax.map(forward_group, (panels, cols, vals)).reshape(NODES, H)
    proj4 = projected.reshape(N_DOM, N_REP, ROWS_DEV, H)
    sends = send_rows.reshape(N_DOM, N_REP, N_DOM, B)
    sent = jax.vmap(jax.vmap(lambda rows_here, index: rows_here[index]))(proj4, sends)
    received = sent.transpose(2, 1, 0, 3, 4).reshape(N_DOM, N_REP, N_DOM * B, H)
    adj4 = bnd_adj.reshape(N_DOM, N_REP, ROWS_DEV, N_DOM * B)
    boundary = jnp.einsum("prij,prjh->prih", adj4.astype(jnp.float32), received.astype(jnp.float32))
    pre = local + boundary.reshape(NODES, H)
    output = jax.nn.silu(pre).astype(jnp.bfloat16)
    sig = jax.nn.sigmoid(pre)
    grad_pre = (cotangent.astype(jnp.float32) * sig * (1.0 + pre * (1.0 - sig))).astype(jnp.bfloat16)
    grad_tiles = grad_pre.reshape(N_DOM, group_tiles, 128, H)

    def backward_group(items):
        col, val, grad = items
        terms = jnp.einsum("tkji,tih->tkjh", val.astype(jnp.float32), grad.astype(jnp.float32))
        onehot = (col[None, :, :] == jnp.arange(group_tiles, dtype=jnp.int32)[:, None, None]).astype(jnp.float32)
        return jnp.einsum("ctk,tkjh->cjh", onehot, terms)

    grad_local = lax.map(backward_group, (cols, vals, grad_tiles)).reshape(NODES, H)
    grad4 = grad_pre.reshape(N_DOM, N_REP, ROWS_DEV, H)
    grad_received = jnp.einsum("prij,prih->prjh", adj4.astype(jnp.float32), grad4.astype(jnp.float32)).astype(jnp.bfloat16)
    returned = grad_received.reshape(N_DOM, N_REP, N_DOM, B, H).transpose(2, 1, 0, 3, 4).reshape(N_DOM, N_REP, N_DOM * B, H)
    flat_sends = sends.reshape(N_DOM, N_REP, N_DOM * B)
    onehot_rows = (jnp.arange(ROWS_DEV, dtype=jnp.int32)[None, None, :, None] == flat_sends[:, :, None, :]).astype(jnp.float32)
    grad_boundary = jnp.einsum("qrim,qrmh->qrih", onehot_rows, returned.astype(jnp.float32)).reshape(NODES, H)
    grad_projected = (grad_local + grad_boundary).astype(jnp.bfloat16)
    grad_features = jnp.dot(grad_projected, weight.T, preferred_element_type=jnp.float32).astype(jnp.bfloat16)
    grad_weight = jnp.dot(features.T, grad_projected, preferred_element_type=jnp.float32)
    return output, grad_features, grad_weight
```

```python
import functools

import jax
import jax.numpy as jnp
from jax import lax
from jax.experimental import pallas as pl
from jax.experimental.pallas import tpu as pltpu
from jax.sharding import PartitionSpec as P

TILE = 128
F32 = jnp.float32
BF16 = jnp.bfloat16
VMEM = pl.BlockSpec(memory_space=pltpu.VMEM)
SMEM = pl.BlockSpec(memory_space=pltpu.SMEM)


def dot(a, b, contract_a, contract_b):
    return lax.dot_general(
        a, b, (((contract_a,), (contract_b,)), ((), ())), preferred_element_type=F32
    )


def wanted_rows(index_ref, rows):
    groups = index_ref.shape[1]
    flat = jnp.concatenate([index_ref[0, q : q + 1, :] for q in range(groups)], axis=1)
    at = lax.broadcasted_iota(jnp.int32, (rows, flat.shape[1]), 0)
    return jnp.where(at == flat, 1.0, 0.0).astype(BF16)


def pick_kernel(index_ref, features_ref, out_ref):
    onehot = wanted_rows(index_ref, features_ref.shape[0])
    picked = dot(onehot, features_ref[...], 0, 0).astype(BF16)
    each = out_ref.shape[1]
    for q in range(out_ref.shape[0]):
        out_ref[q] = picked[q * each : (q + 1) * each]


def layer_kernel(rep, cols_ref, counts_ref, vals_ref, received_ref, bnd_ref, cot_ref, weight_ref, *refs):
    blocks = refs[:rep]
    out_ref, own_ref = refs[rep], refs[rep + 1]
    sends = refs[rep + 2 : 2 * rep + 1]
    message_ref, panel, terms = refs[2 * rep + 1 :]
    me = lax.axis_index("rep")
    tiles, slots = cols_ref.shape
    width = weight_ref.shape[1]
    for shift, block in enumerate(blocks):
        owner = lax.rem(me - shift + rep, rep)
        for t in range(tiles):
            panel[owner * tiles + t] = block[t * TILE : (t + 1) * TILE, :]
    groups, each = received_ref.shape[0], received_ref.shape[1]
    received = jnp.concatenate([received_ref[q] for q in range(groups)], axis=0)
    adjacency = []
    forward = []
    backward = []
    for t in range(tiles):
        live = [
            jnp.where(k < counts_ref[t], vals_ref[t, k], jnp.zeros_like(vals_ref[t, k]))
            for k in range(slots)
        ]
        chosen = jnp.concatenate([panel[cols_ref[t, k]] for k in range(slots)], axis=0)
        stacked = jnp.concatenate(live, axis=0)
        adjacency.append(stacked)
        forward.append(dot(jnp.concatenate(live, axis=1), chosen, 1, 0))
        backward.append(dot(stacked, chosen, 0, 0))
    outside = dot(bnd_ref[...], received, 1, 0)
    mixed = jnp.concatenate(forward, axis=0) + outside
    turned = (jnp.concatenate(backward, axis=0) + outside).astype(BF16)
    high = mixed.astype(BF16)
    low = (mixed - high.astype(F32)).astype(BF16)
    weight = weight_ref[...]
    pre = dot(high, weight, 1, 0) + dot(low, weight, 1, 0)
    sig = jax.nn.sigmoid(pre)
    out_ref[...] = (pre * sig).astype(BF16)
    grad = (cot_ref[...].astype(F32) * sig * (1.0 + pre * (1.0 - sig))).astype(BF16)
    terms[...] = jnp.zeros_like(terms)
    for t in range(tiles):
        parts = dot(adjacency[t], grad[t * TILE : (t + 1) * TILE], 1, 0)
        for k in range(slots):
            terms[cols_ref[t, k]] += parts[k * TILE : (k + 1) * TILE]
    for t in range(tiles):
        own_ref[t * TILE : (t + 1) * TILE, :] = terms[me * tiles + t]
        for shift, send in enumerate(sends, 1):
            owner = lax.rem(me + shift, rep)
            send[t * TILE : (t + 1) * TILE, :] = terms[owner * tiles + t].astype(BF16)
    boundary = dot(bnd_ref[...], grad, 0, 0).astype(BF16)
    partial = dot(turned, grad, 0, 0).astype(BF16)
    share = partial.shape[0] // groups
    for q in range(groups):
        message_ref[q, :each, :] = boundary[q * each : (q + 1) * each]
        message_ref[q, each:, :] = partial[q * share : (q + 1) * share]


def final_kernel(index_ref, returned_ref, weight_ref, own_ref, *refs):
    arrived, out_ref = refs[:-1], refs[-1]
    groups, each = index_ref.shape[1], index_ref.shape[2]
    onehot = wanted_rows(index_ref, own_ref.shape[0])
    returned = jnp.concatenate([returned_ref[q, :each, :] for q in range(groups)], axis=0)
    total = own_ref[...] + dot(onehot, returned, 1, 0)
    for term in arrived:
        total = total + term[...].astype(F32)
    out_ref[...] = dot(total.astype(BF16), weight_ref[...], 1, 1).astype(BF16)


def body(features, weight, tile_cols, tile_vals, tile_counts, send_rows, bnd_adj, cotangent):
    rows, feats = features.shape
    width = weight.shape[1]
    tiles, slots = tile_cols.shape
    groups, each = send_rows.shape[1], send_rows.shape[2]
    rep = lax.axis_size("rep")
    share = feats // groups
    params = pltpu.CompilerParams(vmem_limit_bytes=40 * 1024 * 1024)

    def shifted(value, shift):
        return lax.ppermute(value, "rep", [(i, (i + shift) % rep) for i in range(rep)])

    blocks = [features] + [shifted(features, shift) for shift in range(1, rep)]
    outgoing = pl.pallas_call(
        pick_kernel,
        out_shape=jax.ShapeDtypeStruct((groups, each, feats), BF16),
        in_specs=[VMEM] * 2,
        out_specs=VMEM,
        compiler_params=params,
        name="pick_rows",
    )(send_rows, features)
    received = lax.all_to_all(outgoing, "dom", split_axis=0, concat_axis=0, tiled=True)
    results = pl.pallas_call(
        functools.partial(layer_kernel, rep),
        out_shape=[
            jax.ShapeDtypeStruct((rows, width), BF16),
            jax.ShapeDtypeStruct((rows, width), F32),
            *[jax.ShapeDtypeStruct((rows, width), BF16)] * (rep - 1),
            jax.ShapeDtypeStruct((groups, each + share, width), BF16),
        ],
        in_specs=[SMEM] * 2 + [VMEM] * (5 + rep),
        out_specs=[VMEM] * (rep + 2),
        scratch_shapes=[
            pltpu.VMEM((rep * tiles, TILE, feats), BF16),
            pltpu.VMEM((rep * tiles, TILE, width), F32),
        ],
        compiler_params=params,
        name="layer",
    )(tile_cols, tile_counts, tile_vals, received, bnd_adj, cotangent, weight, *blocks)
    output, own, sends, message = results[0], results[1], results[2:-1], results[-1]
    returned = lax.all_to_all(message, "dom", split_axis=0, concat_axis=0, tiled=True)
    arrived = [shifted(send, shift) for shift, send in enumerate(sends, 1)]
    chunk = jnp.sum(returned[:, each:].astype(F32), axis=0).astype(BF16)
    if rep == 4:
        one, two, three = [shifted(chunk, shift).astype(F32) for shift in (1, 2, 3)]
        total = (chunk.astype(F32) + two) + (one + three)
    else:
        total = jnp.sum(lax.all_gather(chunk, "rep").astype(F32), axis=0)
    spread = jnp.broadcast_to(total.astype(BF16)[None], (groups, share, width))
    grad_weight = lax.all_to_all(spread, "dom", split_axis=0, concat_axis=0, tiled=True)
    grad_weight = grad_weight.reshape(feats, width).astype(F32)
    grad_features = pl.pallas_call(
        final_kernel,
        out_shape=jax.ShapeDtypeStruct((rows, feats), BF16),
        in_specs=[VMEM] * (3 + rep),
        out_specs=VMEM,
        compiler_params=params,
        name="input_gradient",
    )(send_rows, returned, weight, own, *arrived)
    return (output, grad_features, grad_weight)


def solution(mesh):
    placed = (
        P(("dom", "rep"), None),
        P(),
        P(("dom", "rep"), None),
        P(("dom", "rep"), None, None, None),
        P(("dom", "rep")),
        P(("dom", "rep"), None, None),
        P(("dom", "rep"), None),
        P(("dom", "rep"), None),
    )
    return jax.shard_map(
        body,
        mesh=mesh,
        in_specs=placed,
        out_specs=(P(("dom", "rep"), None), P(("dom", "rep"), None), P()),
        check_vma=False,
    )
```

```python
import functools

import jax
import jax.numpy as jnp
from jax import lax
from jax.experimental import pallas as pl
from jax.experimental.pallas import tpu as pltpu
from jax.sharding import PartitionSpec as P

TILE = 128
F32 = jnp.float32
BF16 = jnp.bfloat16
VMEM = pl.BlockSpec(memory_space=pltpu.VMEM)
HBM = pl.BlockSpec(memory_space=pltpu.HBM)
SMEM = pl.BlockSpec(memory_space=pltpu.SMEM)


def dot(a, b, contract_a, contract_b):
    return lax.dot_general(
        a, b, (((contract_a,), (contract_b,)), ((), ())), preferred_element_type=F32
    )


def target(me, shift, count):
    return me ^ shift if count & (count - 1) == 0 else (me + shift) % count


def source(me, shift, count):
    return me ^ shift if count & (count - 1) == 0 else (me - shift + count) % count


def wanted_rows(index_ref, rows):
    groups = index_ref.shape[1]
    flat = jnp.concatenate([index_ref[0, q : q + 1, :] for q in range(groups)], axis=1)
    at = lax.broadcasted_iota(jnp.int32, (rows, flat.shape[1]), 0)
    return jnp.where(at == flat, 1.0, 0.0).astype(BF16)


def pick_kernel(index_ref, features_ref, vals_ref, cot_ref, out_ref, vals_out, cot_out, index, features, sems):
    copies = [
        pltpu.make_async_copy(index_ref, index, sems.at[0]),
        pltpu.make_async_copy(features_ref, features, sems.at[1]),
        pltpu.make_async_copy(cot_ref, cot_out, sems.at[2]),
        pltpu.make_async_copy(vals_ref, vals_out, sems.at[3]),
    ]
    for copy in copies:
        copy.start()
    copies[0].wait()
    onehot = wanted_rows(index, features_ref.shape[0])
    copies[1].wait()
    picked = dot(onehot, features[...], 0, 0).astype(BF16)
    each = out_ref.shape[1]
    for q in range(out_ref.shape[0]):
        out_ref[q] = picked[q * each : (q + 1) * each]
    for copy in copies[2:]:
        copy.wait()


def layer_kernel(rep, cols_ref, counts_ref, vals_ref, received_ref, bnd_ref, cot_ref, weight_ref, *refs):
    blocks = refs[:rep]
    out_ref, own_ref = refs[rep], refs[rep + 1]
    sends = refs[rep + 2 : 2 * rep + 1]
    message_ref, panel, terms = refs[2 * rep + 1 :]
    me = lax.axis_index("rep")
    tiles, slots = cols_ref.shape
    width = weight_ref.shape[1]
    for shift, block in enumerate(blocks):
        owner = source(me, shift, rep)
        for t in range(tiles):
            panel[owner * tiles + t] = block[t * TILE : (t + 1) * TILE, :]
    groups, each = received_ref.shape[0], received_ref.shape[1]
    received = jnp.concatenate([received_ref[q] for q in range(groups)], axis=0)
    adjacency = []
    forward = []
    backward = []
    for t in range(tiles):
        live = [
            jnp.where(k < counts_ref[t], vals_ref[t, k], jnp.zeros_like(vals_ref[t, k]))
            for k in range(slots)
        ]
        chosen = jnp.concatenate([panel[cols_ref[t, k]] for k in range(slots)], axis=0)
        stacked = jnp.concatenate(live, axis=0)
        adjacency.append(stacked)
        forward.append(dot(jnp.concatenate(live, axis=1), chosen, 1, 0))
        backward.append(dot(stacked, chosen, 0, 0))
    outside = dot(bnd_ref[...], received, 1, 0)
    mixed = jnp.concatenate(forward, axis=0) + outside
    turned = (jnp.concatenate(backward, axis=0) + outside).astype(BF16)
    high = mixed.astype(BF16)
    low = (mixed - high.astype(F32)).astype(BF16)
    weight = weight_ref[...]
    pre = dot(high, weight, 1, 0) + dot(low, weight, 1, 0)
    sig = jax.nn.sigmoid(pre)
    out_ref[...] = (pre * sig).astype(BF16)
    grad = (cot_ref[...].astype(F32) * sig * (1.0 + pre * (1.0 - sig))).astype(BF16)
    terms[...] = jnp.zeros_like(terms)
    for t in range(tiles):
        parts = dot(adjacency[t], grad[t * TILE : (t + 1) * TILE], 1, 0)
        for k in range(slots):
            terms[cols_ref[t, k]] += parts[k * TILE : (k + 1) * TILE]
    for t in range(tiles):
        own_ref[t * TILE : (t + 1) * TILE, :] = terms[me * tiles + t]
        for shift, send in enumerate(sends, 1):
            owner = target(me, shift, rep)
            send[t * TILE : (t + 1) * TILE, :] = terms[owner * tiles + t].astype(BF16)
    boundary = dot(bnd_ref[...], grad, 0, 0).astype(BF16)
    partial = dot(turned, grad, 0, 0).astype(BF16)
    share = partial.shape[0] // groups
    for q in range(groups):
        message_ref[q, :each, :] = boundary[q * each : (q + 1) * each]
        message_ref[q, each:, :] = partial[q * share : (q + 1) * share]


def final_kernel(index_ref, returned_ref, weight_ref, own_ref, *refs):
    arrived, out_ref = refs[:-1], refs[-1]
    groups, each = index_ref.shape[1], index_ref.shape[2]
    onehot = wanted_rows(index_ref, own_ref.shape[0])
    returned = jnp.concatenate([returned_ref[q, :each, :] for q in range(groups)], axis=0)
    total = own_ref[...] + dot(onehot, returned, 1, 0)
    for term in arrived:
        total = total + term[...].astype(F32)
    out_ref[...] = dot(total.astype(BF16), weight_ref[...], 1, 1).astype(BF16)


def body(features, weight, tile_cols, tile_vals, tile_counts, send_rows, bnd_adj, cotangent):
    rows, feats = features.shape
    width = weight.shape[1]
    tiles, slots = tile_cols.shape
    groups, each = send_rows.shape[1], send_rows.shape[2]
    rep = lax.axis_size("rep")
    share = feats // groups
    params = pltpu.CompilerParams(vmem_limit_bytes=40 * 1024 * 1024)

    def shifted(value, shift):
        return lax.ppermute(value, "rep", [(i, target(i, shift, rep)) for i in range(rep)])

    blocks = [features] + [shifted(features, shift) for shift in range(1, rep)]
    outgoing, tile_vals, cotangent = pl.pallas_call(
        pick_kernel,
        out_shape=[
            jax.ShapeDtypeStruct((groups, each, feats), BF16),
            jax.ShapeDtypeStruct(tile_vals.shape, BF16),
            jax.ShapeDtypeStruct(cotangent.shape, BF16),
        ],
        in_specs=[HBM] * 4,
        out_specs=[VMEM] * 3,
        scratch_shapes=[
            pltpu.VMEM(send_rows.shape, jnp.int32),
            pltpu.VMEM((rows, feats), BF16),
            pltpu.SemaphoreType.DMA((4,)),
        ],
        compiler_params=params,
        name="pick_rows",
    )(send_rows, features, tile_vals, cotangent)
    received = lax.all_to_all(outgoing, "dom", split_axis=0, concat_axis=0, tiled=True)
    results = pl.pallas_call(
        functools.partial(layer_kernel, rep),
        out_shape=[
            jax.ShapeDtypeStruct((rows, width), BF16),
            jax.ShapeDtypeStruct((rows, width), F32),
            *[jax.ShapeDtypeStruct((rows, width), BF16)] * (rep - 1),
            jax.ShapeDtypeStruct((groups, each + share, width), BF16),
        ],
        in_specs=[SMEM] * 2 + [VMEM] * (5 + rep),
        out_specs=[VMEM] * (rep + 2),
        scratch_shapes=[
            pltpu.VMEM((rep * tiles, TILE, feats), BF16),
            pltpu.VMEM((rep * tiles, TILE, width), F32),
        ],
        compiler_params=params,
        name="layer",
    )(tile_cols, tile_counts, tile_vals, received, bnd_adj, cotangent, weight, *blocks)
    output, own, sends, message = results[0], results[1], results[2:-1], results[-1]
    returned = lax.all_to_all(message, "dom", split_axis=0, concat_axis=0, tiled=True)
    arrived = [shifted(send, shift) for shift, send in enumerate(sends, 1)]
    chunk = jnp.sum(returned[:, each:].astype(F32), axis=0).astype(BF16)
    chunks = lax.all_gather(chunk, ("dom", "rep"), axis=0).reshape(groups, rep, share, width)
    grad_weight = jnp.sum(chunks.astype(F32), axis=1).reshape(feats, width)
    grad_features = pl.pallas_call(
        final_kernel,
        out_shape=jax.ShapeDtypeStruct((rows, feats), BF16),
        in_specs=[VMEM] * (3 + rep),
        out_specs=VMEM,
        compiler_params=params,
        name="input_gradient",
    )(send_rows, returned, weight, own, *arrived)
    return (output, grad_features, grad_weight)


def solution(mesh):
    placed = (
        P(("dom", "rep"), None),
        P(),
        P(("dom", "rep"), None),
        P(("dom", "rep"), None, None, None),
        P(("dom", "rep")),
        P(("dom", "rep"), None, None),
        P(("dom", "rep"), None),
        P(("dom", "rep"), None),
    )
    return jax.shard_map(
        body,
        mesh=mesh,
        in_specs=placed,
        out_specs=(P(("dom", "rep"), None), P(("dom", "rep"), None), P()),
        check_vma=False,
    )
```

```python
import functools

import jax
import jax.numpy as jnp
from jax import lax
from jax.experimental import pallas as pl
from jax.experimental.pallas import tpu as pltpu
from jax.sharding import PartitionSpec as P

TILE = 128
F32 = jnp.float32
BF16 = jnp.bfloat16
VMEM = pl.BlockSpec(memory_space=pltpu.VMEM)
HBM = pl.BlockSpec(memory_space=pltpu.HBM)
SMEM = pl.BlockSpec(memory_space=pltpu.SMEM)


def dot(a, b, contract_a, contract_b):
    return lax.dot_general(
        a, b, (((contract_a,), (contract_b,)), ((), ())), preferred_element_type=F32
    )


def target(me, shift, count):
    return me ^ shift if count & (count - 1) == 0 else (me + shift) % count


def source(me, shift, count):
    return me ^ shift if count & (count - 1) == 0 else (me - shift + count) % count


def share_order(q, groups):
    order = 0
    for b in range(groups.bit_length() - 1):
        order = 2 * order + (q >> b & 1)
    return order


def wanted_rows(index_ref, rows):
    groups = index_ref.shape[1]
    flat = jnp.concatenate([index_ref[0, q : q + 1, :] for q in range(groups)], axis=1)
    at = lax.broadcasted_iota(jnp.int32, (rows, flat.shape[1]), 0)
    return jnp.where(at == flat, 1.0, 0.0).astype(BF16)


def pick_kernel(index_ref, features_ref, vals_ref, cot_ref, out_ref, vals_out, cot_out, index, features, sems):
    copies = [
        pltpu.make_async_copy(index_ref, index, sems.at[0]),
        pltpu.make_async_copy(features_ref, features, sems.at[1]),
        pltpu.make_async_copy(cot_ref, cot_out, sems.at[2]),
        pltpu.make_async_copy(vals_ref, vals_out, sems.at[3]),
    ]
    for copy in copies:
        copy.start()
    copies[0].wait()
    onehot = wanted_rows(index, features_ref.shape[0])
    copies[1].wait()
    picked = dot(onehot, features[...], 0, 0).astype(BF16)
    each = out_ref.shape[1]
    for q in range(out_ref.shape[0]):
        out_ref[q] = picked[q * each : (q + 1) * each]
    for copy in copies[2:]:
        copy.wait()


def layer_kernel(rep, cols_ref, counts_ref, vals_ref, received_ref, bnd_ref, cot_ref, weight_ref, *refs):
    blocks = refs[:rep]
    out_ref, own_ref = refs[rep], refs[rep + 1]
    sends = refs[rep + 2 : 2 * rep + 1]
    message_ref, panel, terms = refs[2 * rep + 1 :]
    me = lax.axis_index("rep")
    tiles, slots = cols_ref.shape
    width = weight_ref.shape[1]
    for shift, block in enumerate(blocks):
        owner = source(me, shift, rep)
        for t in range(tiles):
            panel[owner * tiles + t] = block[t * TILE : (t + 1) * TILE, :]
    groups, each = received_ref.shape[0], received_ref.shape[1]
    received = jnp.concatenate([received_ref[q] for q in range(groups)], axis=0)
    adjacency = []
    forward = []
    backward = []
    for t in range(tiles):
        live = [
            jnp.where(k < counts_ref[t], vals_ref[t, k], jnp.zeros_like(vals_ref[t, k]))
            for k in range(slots)
        ]
        chosen = jnp.concatenate([panel[cols_ref[t, k]] for k in range(slots)], axis=0)
        stacked = jnp.concatenate(live, axis=0)
        adjacency.append(stacked)
        forward.append(dot(jnp.concatenate(live, axis=1), chosen, 1, 0))
        backward.append(dot(stacked, chosen, 0, 0))
    outside = dot(bnd_ref[...], received, 1, 0)
    mixed = jnp.concatenate(forward, axis=0) + outside
    turned = (jnp.concatenate(backward, axis=0) + outside).astype(BF16)
    high = mixed.astype(BF16)
    low = (mixed - high.astype(F32)).astype(BF16)
    weight = weight_ref[...]
    pre = dot(high, weight, 1, 0) + dot(low, weight, 1, 0)
    sig = jax.nn.sigmoid(pre)
    out_ref[...] = (pre * sig).astype(BF16)
    grad = (cot_ref[...].astype(F32) * sig * (1.0 + pre * (1.0 - sig))).astype(BF16)
    terms[...] = jnp.zeros_like(terms)
    for t in range(tiles):
        parts = dot(adjacency[t], grad[t * TILE : (t + 1) * TILE], 1, 0)
        for k in range(slots):
            terms[cols_ref[t, k]] += parts[k * TILE : (k + 1) * TILE]
    for t in range(tiles):
        own_ref[t * TILE : (t + 1) * TILE, :] = terms[me * tiles + t]
        for shift, send in enumerate(sends, 1):
            owner = target(me, shift, rep)
            send[t * TILE : (t + 1) * TILE, :] = terms[owner * tiles + t].astype(BF16)
    boundary = dot(bnd_ref[...], grad, 0, 0).astype(BF16)
    partial = dot(turned, grad, 0, 0).astype(BF16)
    share = partial.shape[0] // groups
    for q in range(groups):
        message_ref[q, :each, :] = boundary[q * each : (q + 1) * each]
        at = share_order(q, groups) * share
        message_ref[q, each:, :] = partial[at : at + share]


def join_kernel(bit, own_ref, got_ref, out_ref):
    own, got = own_ref[...], got_ref[...]
    half = own.shape[0]
    upper = lax.rem(lax.axis_index("dom") // bit, 2) == 1
    out_ref[:half, :] = jnp.where(upper, got, own).astype(out_ref.dtype)
    out_ref[half:, :] = jnp.where(upper, own, got).astype(out_ref.dtype)


def final_kernel(index_ref, returned_ref, weight_ref, own_ref, *refs):
    arrived, out_ref = refs[:-1], refs[-1]
    groups, each = index_ref.shape[1], index_ref.shape[2]
    onehot = wanted_rows(index_ref, own_ref.shape[0])
    returned = jnp.concatenate([returned_ref[q, :each, :] for q in range(groups)], axis=0)
    total = own_ref[...] + dot(onehot, returned, 1, 0)
    for term in arrived:
        total = total + term[...].astype(F32)
    out_ref[...] = dot(total.astype(BF16), weight_ref[...], 1, 1).astype(BF16)


def body(features, weight, tile_cols, tile_vals, tile_counts, send_rows, bnd_adj, cotangent):
    rows, feats = features.shape
    width = weight.shape[1]
    tiles, slots = tile_cols.shape
    groups, each = send_rows.shape[1], send_rows.shape[2]
    rep = lax.axis_size("rep")
    share = feats // groups
    bits = [1 << b for b in range(groups.bit_length() - 1)]
    params = pltpu.CompilerParams(vmem_limit_bytes=40 * 1024 * 1024)

    def shifted(value, shift):
        return lax.ppermute(value, "rep", [(i, target(i, shift, rep)) for i in range(rep)])

    blocks = [features] + [shifted(features, shift) for shift in range(1, rep)]
    outgoing, tile_vals, cotangent = pl.pallas_call(
        pick_kernel,
        out_shape=[
            jax.ShapeDtypeStruct((groups, each, feats), BF16),
            jax.ShapeDtypeStruct(tile_vals.shape, BF16),
            jax.ShapeDtypeStruct(cotangent.shape, BF16),
        ],
        in_specs=[HBM] * 4,
        out_specs=[VMEM] * 3,
        scratch_shapes=[
            pltpu.VMEM(send_rows.shape, jnp.int32),
            pltpu.VMEM((rows, feats), BF16),
            pltpu.SemaphoreType.DMA((4,)),
        ],
        compiler_params=params,
        name="pick_rows",
    )(*[pltpu.with_memory_space_constraint(x, pltpu.HBM) for x in (send_rows, features, tile_vals, cotangent)])
    received = lax.all_to_all(outgoing, "dom", split_axis=0, concat_axis=0, tiled=True)
    results = pl.pallas_call(
        functools.partial(layer_kernel, rep),
        out_shape=[
            jax.ShapeDtypeStruct((rows, width), BF16),
            jax.ShapeDtypeStruct((rows, width), F32),
            *[jax.ShapeDtypeStruct((rows, width), BF16)] * (rep - 1),
            jax.ShapeDtypeStruct((groups, each + share, width), BF16),
        ],
        in_specs=[SMEM] * 2 + [VMEM] * (5 + rep),
        out_specs=[VMEM] * (rep + 2),
        scratch_shapes=[
            pltpu.VMEM((rep * tiles, TILE, feats), BF16),
            pltpu.VMEM((rep * tiles, TILE, width), F32),
        ],
        compiler_params=params,
        name="layer",
    )(tile_cols, tile_counts, tile_vals, received, bnd_adj, cotangent, weight, *blocks)
    output, own, sends, message = results[0], results[1], results[2:-1], results[-1]
    returned = lax.all_to_all(message, "dom", split_axis=0, concat_axis=0, tiled=True)
    arrived = [shifted(send, shift) for shift, send in enumerate(sends, 1)]
    chunk = jnp.sum(returned[:, each:].astype(F32), axis=0).astype(BF16)
    if rep == 4:
        one, two, three = [shifted(chunk, shift).astype(F32) for shift in (1, 2, 3)]
        total = (chunk.astype(F32) + two) + (one + three)
    else:
        total = jnp.sum(lax.all_gather(chunk, "rep").astype(F32), axis=0)
    piece = total.astype(BF16)
    for bit in reversed(bits):
        got = lax.ppermute(piece, "dom", [(i, i ^ bit) for i in range(groups)])
        piece = pl.pallas_call(
            functools.partial(join_kernel, bit),
            out_shape=jax.ShapeDtypeStruct((2 * piece.shape[0], width), F32 if bit == 1 else BF16),
            in_specs=[VMEM] * 2,
            out_specs=VMEM,
            compiler_params=params,
            cost_estimate=pl.CostEstimate(flops=1, bytes_accessed=1, transcendentals=0),
            name="join",
        )(piece, got)
    grad_weight = piece
    grad_features = pl.pallas_call(
        final_kernel,
        out_shape=jax.ShapeDtypeStruct((rows, feats), BF16),
        in_specs=[VMEM] * (3 + rep),
        out_specs=VMEM,
        compiler_params=params,
        name="input_gradient",
    )(send_rows, returned, weight, own, *arrived)
    return (output, grad_features, grad_weight)


def solution(mesh):
    placed = (
        P(("dom", "rep"), None),
        P(),
        P(("dom", "rep"), None),
        P(("dom", "rep"), None, None, None),
        P(("dom", "rep")),
        P(("dom", "rep"), None, None),
        P(("dom", "rep"), None),
        P(("dom", "rep"), None),
    )
    return jax.shard_map(
        body,
        mesh=mesh,
        in_specs=placed,
        out_specs=(P(("dom", "rep"), None), P(("dom", "rep"), None), P()),
        check_vma=False,
    )
```

```python
import functools

import jax
import jax.numpy as jnp
from jax import lax
from jax.experimental import pallas as pl
from jax.experimental.pallas import tpu as pltpu
from jax.sharding import PartitionSpec as P

TILE = 128
F32 = jnp.float32
BF16 = jnp.bfloat16
VMEM = pl.BlockSpec(memory_space=pltpu.VMEM)
HBM = pl.BlockSpec(memory_space=pltpu.HBM)
SMEM = pl.BlockSpec(memory_space=pltpu.SMEM)


def dot(a, b, contract_a, contract_b):
    return lax.dot_general(
        a, b, (((contract_a,), (contract_b,)), ((), ())), preferred_element_type=F32
    )


def target(me, shift, count):
    return me ^ shift if count & (count - 1) == 0 else (me + shift) % count


def source(me, shift, count):
    return me ^ shift if count & (count - 1) == 0 else (me - shift + count) % count


def share_order(q, groups):
    order = 0
    for b in range(groups.bit_length() - 1):
        order = 2 * order + (q >> b & 1)
    return order


def wanted_rows(index_ref, rows):
    groups = index_ref.shape[1]
    flat = jnp.concatenate([index_ref[0, q : q + 1, :] for q in range(groups)], axis=1)
    at = lax.broadcasted_iota(jnp.int32, (rows, flat.shape[1]), 0)
    return jnp.where(at == flat, 1.0, 0.0).astype(BF16)


def pick_kernel(index_ref, features_ref, vals_ref, cot_ref, out_ref, vals_out, cot_out, index, features, sems):
    copies = [
        pltpu.make_async_copy(index_ref, index, sems.at[0]),
        pltpu.make_async_copy(features_ref, features, sems.at[1]),
        pltpu.make_async_copy(cot_ref, cot_out, sems.at[2]),
        pltpu.make_async_copy(vals_ref, vals_out, sems.at[3]),
    ]
    for copy in copies:
        copy.start()
    copies[0].wait()
    onehot = wanted_rows(index, features_ref.shape[0])
    copies[1].wait()
    picked = dot(onehot, features[...], 0, 0).astype(BF16)
    each = out_ref.shape[1]
    for q in range(out_ref.shape[0]):
        out_ref[q] = picked[q * each : (q + 1) * each]
    for copy in copies[2:]:
        copy.wait()


def layer_kernel(rep, cols_ref, counts_ref, vals_ref, received_ref, bnd_ref, cot_ref, weight_ref, *refs):
    blocks = refs[:rep]
    out_ref, own_ref = refs[rep], refs[rep + 1]
    sends = refs[rep + 2 : 2 * rep + 1]
    message_ref, panel, terms = refs[2 * rep + 1 :]
    me = lax.axis_index("rep")
    tiles, slots = cols_ref.shape
    width = weight_ref.shape[1]
    for shift, block in enumerate(blocks):
        owner = source(me, shift, rep)
        for t in range(tiles):
            panel[owner * tiles + t] = block[t * TILE : (t + 1) * TILE, :]
    groups, each = received_ref.shape[0], received_ref.shape[1]
    received = jnp.concatenate([received_ref[q] for q in range(groups)], axis=0)
    adjacency = []
    forward = []
    backward = []
    for t in range(tiles):
        live = [
            jnp.where(k < counts_ref[t], vals_ref[t, k], jnp.zeros_like(vals_ref[t, k]))
            for k in range(slots)
        ]
        chosen = jnp.concatenate([panel[cols_ref[t, k]] for k in range(slots)], axis=0)
        stacked = jnp.concatenate(live, axis=0)
        adjacency.append(stacked)
        forward.append(dot(jnp.concatenate(live, axis=1), chosen, 1, 0))
        backward.append(dot(stacked, chosen, 0, 0))
    outside = dot(bnd_ref[...], received, 1, 0)
    mixed = jnp.concatenate(forward, axis=0) + outside
    turned = (jnp.concatenate(backward, axis=0) + outside).astype(BF16)
    high = mixed.astype(BF16)
    low = (mixed - high.astype(F32)).astype(BF16)
    weight = weight_ref[...]
    pre = dot(high, weight, 1, 0) + dot(low, weight, 1, 0)
    sig = jax.nn.sigmoid(pre)
    out_ref[...] = (pre * sig).astype(BF16)
    grad = (cot_ref[...].astype(F32) * sig * (1.0 + pre * (1.0 - sig))).astype(BF16)
    terms[...] = jnp.zeros_like(terms)
    for t in range(tiles):
        parts = dot(adjacency[t], grad[t * TILE : (t + 1) * TILE], 1, 0)
        for k in range(slots):
            terms[cols_ref[t, k]] += parts[k * TILE : (k + 1) * TILE]
    for t in range(tiles):
        own_ref[t * TILE : (t + 1) * TILE, :] = terms[me * tiles + t]
        for shift, send in enumerate(sends, 1):
            owner = target(me, shift, rep)
            send[t * TILE : (t + 1) * TILE, :] = terms[owner * tiles + t].astype(BF16)
    boundary = dot(bnd_ref[...], grad, 0, 0).astype(BF16)
    partial = dot(turned, grad, 0, 0).astype(BF16)
    share = partial.shape[0] // groups
    for q in range(groups):
        message_ref[q, :each, :] = boundary[q * each : (q + 1) * each]
        at = share_order(q, groups) * share
        message_ref[q, each:, :] = partial[at : at + share]


def rep_sum_kernel(*refs):
    chunk, one, two, three = [ref[...].astype(F32) for ref in refs[:4]]
    refs[-1][...] = ((chunk + two) + (one + three)).astype(BF16)


def join_kernel(bit, own_ref, got_ref, out_ref):
    own, got = own_ref[...], got_ref[...]
    half = own.shape[0]
    upper = lax.rem(lax.axis_index("dom") // bit, 2) == 1
    out_ref[:half, :] = jnp.where(upper, got, own).astype(out_ref.dtype)
    out_ref[half:, :] = jnp.where(upper, own, got).astype(out_ref.dtype)


def final_kernel(index_ref, returned_ref, weight_ref, own_ref, *refs):
    arrived, out_ref = refs[:-1], refs[-1]
    groups, each = index_ref.shape[1], index_ref.shape[2]
    onehot = wanted_rows(index_ref, own_ref.shape[0])
    returned = jnp.concatenate([returned_ref[q, :each, :] for q in range(groups)], axis=0)
    total = own_ref[...] + dot(onehot, returned, 1, 0)
    for term in arrived:
        total = total + term[...].astype(F32)
    out_ref[...] = dot(total.astype(BF16), weight_ref[...], 1, 1).astype(BF16)


def body(features, weight, tile_cols, tile_vals, tile_counts, send_rows, bnd_adj, cotangent):
    rows, feats = features.shape
    width = weight.shape[1]
    tiles, slots = tile_cols.shape
    groups, each = send_rows.shape[1], send_rows.shape[2]
    rep = lax.axis_size("rep")
    share = feats // groups
    bits = [1 << b for b in range(groups.bit_length() - 1)]
    params = pltpu.CompilerParams(vmem_limit_bytes=40 * 1024 * 1024)

    def shifted(value, shift):
        return lax.ppermute(value, "rep", [(i, target(i, shift, rep)) for i in range(rep)])

    blocks = [features] + [shifted(features, shift) for shift in range(1, rep)]
    outgoing, tile_vals, cotangent = pl.pallas_call(
        pick_kernel,
        out_shape=[
            jax.ShapeDtypeStruct((groups, each, feats), BF16),
            jax.ShapeDtypeStruct(tile_vals.shape, BF16),
            jax.ShapeDtypeStruct(cotangent.shape, BF16),
        ],
        in_specs=[HBM] * 4,
        out_specs=[VMEM] * 3,
        scratch_shapes=[
            pltpu.VMEM(send_rows.shape, jnp.int32),
            pltpu.VMEM((rows, feats), BF16),
            pltpu.SemaphoreType.DMA((4,)),
        ],
        compiler_params=params,
        name="pick_rows",
    )(*[pltpu.with_memory_space_constraint(x, pltpu.HBM) for x in (send_rows, features, tile_vals, cotangent)])
    received = lax.all_to_all(outgoing, "dom", split_axis=0, concat_axis=0, tiled=True)
    results = pl.pallas_call(
        functools.partial(layer_kernel, rep),
        out_shape=[
            jax.ShapeDtypeStruct((rows, width), BF16),
            jax.ShapeDtypeStruct((rows, width), F32),
            *[jax.ShapeDtypeStruct((rows, width), BF16)] * (rep - 1),
            jax.ShapeDtypeStruct((groups, each + share, width), BF16),
        ],
        in_specs=[SMEM] * 2 + [VMEM] * (5 + rep),
        out_specs=[VMEM] * (rep + 2),
        scratch_shapes=[
            pltpu.VMEM((rep * tiles, TILE, feats), BF16),
            pltpu.VMEM((rep * tiles, TILE, width), F32),
        ],
        compiler_params=params,
        name="layer",
    )(tile_cols, tile_counts, tile_vals, received, bnd_adj, cotangent, weight, *blocks)
    output, own, sends, message = results[0], results[1], results[2:-1], results[-1]
    returned = lax.all_to_all(message, "dom", split_axis=0, concat_axis=0, tiled=True)
    arrived = [shifted(send, shift) for shift, send in enumerate(sends, 1)]
    chunk = jnp.sum(returned[:, each:].astype(F32), axis=0).astype(BF16)
    if rep == 4:
        piece = pl.pallas_call(
            rep_sum_kernel,
            out_shape=jax.ShapeDtypeStruct(chunk.shape, BF16),
            in_specs=[VMEM] * (3 + rep),
            out_specs=VMEM,
            compiler_params=params,
            cost_estimate=pl.CostEstimate(flops=1, bytes_accessed=1, transcendentals=0),
            name="rep_sum",
        )(chunk, *[shifted(chunk, shift) for shift in (1, 2, 3)], *arrived)
    else:
        piece = jnp.sum(lax.all_gather(chunk, "rep").astype(F32), axis=0).astype(BF16)
    for bit in reversed(bits):
        got = lax.ppermute(piece, "dom", [(i, i ^ bit) for i in range(groups)])
        piece = pl.pallas_call(
            functools.partial(join_kernel, bit),
            out_shape=jax.ShapeDtypeStruct((2 * piece.shape[0], width), F32 if bit == 1 else BF16),
            in_specs=[VMEM] * 2,
            out_specs=VMEM,
            compiler_params=params,
            cost_estimate=pl.CostEstimate(flops=1, bytes_accessed=1, transcendentals=0),
            name="join",
        )(piece, got)
    grad_weight = piece
    grad_features = pl.pallas_call(
        final_kernel,
        out_shape=jax.ShapeDtypeStruct((rows, feats), BF16),
        in_specs=[VMEM] * (3 + rep),
        out_specs=VMEM,
        compiler_params=params,
        name="input_gradient",
    )(send_rows, returned, weight, own, *arrived)
    return (output, grad_features, grad_weight)


def solution(mesh):
    placed = (
        P(("dom", "rep"), None),
        P(),
        P(("dom", "rep"), None),
        P(("dom", "rep"), None, None, None),
        P(("dom", "rep")),
        P(("dom", "rep"), None, None),
        P(("dom", "rep"), None),
        P(("dom", "rep"), None),
    )
    return jax.shard_map(
        body,
        mesh=mesh,
        in_specs=placed,
        out_specs=(P(("dom", "rep"), None), P(("dom", "rep"), None), P()),
        check_vma=False,
    )
```

```python
import functools

import jax
import jax.numpy as jnp
from jax import lax
from jax.experimental import pallas as pl
from jax.experimental.pallas import tpu as pltpu
from jax.sharding import PartitionSpec as P

TILE = 128
F32 = jnp.float32
BF16 = jnp.bfloat16
VMEM = pl.BlockSpec(memory_space=pltpu.VMEM)
HBM = pl.BlockSpec(memory_space=pltpu.HBM)
SMEM = pl.BlockSpec(memory_space=pltpu.SMEM)


def dot(a, b, contract_a, contract_b):
    return lax.dot_general(
        a, b, (((contract_a,), (contract_b,)), ((), ())), preferred_element_type=F32
    )


def target(me, shift, count):
    return me ^ shift if count & (count - 1) == 0 else (me + shift) % count


def source(me, shift, count):
    return me ^ shift if count & (count - 1) == 0 else (me - shift + count) % count


def wanted_rows(index_ref, rows):
    groups = index_ref.shape[1]
    flat = jnp.concatenate([index_ref[0, q : q + 1, :] for q in range(groups)], axis=1)
    at = lax.broadcasted_iota(jnp.int32, (rows, flat.shape[1]), 0)
    return jnp.where(at == flat, 1.0, 0.0).astype(BF16)


def pick_kernel(index_ref, features_ref, vals_ref, cot_ref, out_ref, vals_out, cot_out, index, features, sems):
    copies = [
        pltpu.make_async_copy(index_ref, index, sems.at[0]),
        pltpu.make_async_copy(features_ref, features, sems.at[1]),
        pltpu.make_async_copy(cot_ref, cot_out, sems.at[2]),
        pltpu.make_async_copy(vals_ref, vals_out, sems.at[3]),
    ]
    for copy in copies:
        copy.start()
    copies[0].wait()
    onehot = wanted_rows(index, features_ref.shape[0])
    copies[1].wait()
    picked = dot(onehot, features[...], 0, 0).astype(BF16)
    each = out_ref.shape[1]
    for q in range(out_ref.shape[0]):
        out_ref[q] = picked[q * each : (q + 1) * each]
    for copy in copies[2:]:
        copy.wait()


def layer_kernel(rep, cols_ref, counts_ref, vals_ref, received_ref, bnd_ref, cot_ref, weight_ref, *refs):
    blocks = refs[:rep]
    out_ref, own_ref = refs[rep], refs[rep + 1]
    sends = refs[rep + 2 : 2 * rep + 1]
    message_ref, partial_ref, panel, terms = refs[2 * rep + 1 :]
    me = lax.axis_index("rep")
    tiles, slots = cols_ref.shape
    width = weight_ref.shape[1]
    for shift, block in enumerate(blocks):
        owner = source(me, shift, rep)
        for t in range(tiles):
            panel[owner * tiles + t] = block[t * TILE : (t + 1) * TILE, :]
    groups, each = received_ref.shape[0], received_ref.shape[1]
    received = jnp.concatenate([received_ref[q] for q in range(groups)], axis=0)
    adjacency = []
    forward = []
    backward = []
    for t in range(tiles):
        live = [
            jnp.where(k < counts_ref[t], vals_ref[t, k], jnp.zeros_like(vals_ref[t, k]))
            for k in range(slots)
        ]
        chosen = jnp.concatenate([panel[cols_ref[t, k]] for k in range(slots)], axis=0)
        stacked = jnp.concatenate(live, axis=0)
        adjacency.append(stacked)
        forward.append(dot(jnp.concatenate(live, axis=1), chosen, 1, 0))
        backward.append(dot(stacked, chosen, 0, 0))
    outside = dot(bnd_ref[...], received, 1, 0)
    mixed = jnp.concatenate(forward, axis=0) + outside
    turned = (jnp.concatenate(backward, axis=0) + outside).astype(BF16)
    high = mixed.astype(BF16)
    low = (mixed - high.astype(F32)).astype(BF16)
    weight = weight_ref[...]
    pre = dot(high, weight, 1, 0) + dot(low, weight, 1, 0)
    sig = jax.nn.sigmoid(pre)
    out_ref[...] = (pre * sig).astype(BF16)
    grad = (cot_ref[...].astype(F32) * sig * (1.0 + pre * (1.0 - sig))).astype(BF16)
    terms[...] = jnp.zeros_like(terms)
    for t in range(tiles):
        parts = dot(adjacency[t], grad[t * TILE : (t + 1) * TILE], 1, 0)
        for k in range(slots):
            terms[cols_ref[t, k]] += parts[k * TILE : (k + 1) * TILE]
    for t in range(tiles):
        own_ref[t * TILE : (t + 1) * TILE, :] = terms[me * tiles + t]
        for shift, send in enumerate(sends, 1):
            owner = target(me, shift, rep)
            send[t * TILE : (t + 1) * TILE, :] = terms[owner * tiles + t].astype(BF16)
    boundary = dot(bnd_ref[...], grad, 0, 0).astype(BF16)
    for q in range(groups):
        message_ref[q] = boundary[q * each : (q + 1) * each]
    partial = dot(turned, grad, 0, 0)
    if partial_ref.shape == partial.shape:
        partial_ref[...] = partial
    else:
        count, high, wide = partial_ref.shape
        across = width // wide
        for j in range(count):
            row, column = j // across * high, j % across * wide
            partial_ref[j] = partial[row : row + high, column : column + wide].astype(BF16)


def sum_kernel(parts_ref, returned_ref, out_ref):
    total = jnp.sum(parts_ref[...].astype(F32), axis=0).astype(BF16)
    out_ref[...] = jnp.broadcast_to(total[None], out_ref.shape)


def spread_kernel(chunks_ref, out_ref):
    count, high, wide = chunks_ref.shape
    across = out_ref.shape[1] // wide
    for j in range(count):
        row, column = j // across * high, j % across * wide
        out_ref[row : row + high, column : column + wide] = chunks_ref[j].astype(F32)


def final_kernel(index_ref, returned_ref, weight_ref, own_ref, *refs):
    arrived, out_ref = refs[:-1], refs[-1]
    groups, each = index_ref.shape[1], index_ref.shape[2]
    onehot = wanted_rows(index_ref, own_ref.shape[0])
    returned = jnp.concatenate([returned_ref[q] for q in range(groups)], axis=0)
    total = own_ref[...] + dot(onehot, returned, 1, 0)
    for term in arrived:
        total = total + term[...].astype(F32)
    out_ref[...] = dot(total.astype(BF16), weight_ref[...], 1, 1).astype(BF16)


def body(features, weight, tile_cols, tile_vals, tile_counts, send_rows, bnd_adj, cotangent):
    rows, feats = features.shape
    width = weight.shape[1]
    tiles, slots = tile_cols.shape
    groups, each = send_rows.shape[1], send_rows.shape[2]
    rep = lax.axis_size("rep")
    devices = groups * rep
    wide = feats * width // (16 * devices)
    chunked = wide >= TILE and width % wide == 0 and feats % 16 == 0
    if chunked:
        partial_shape = jax.ShapeDtypeStruct((devices, 16, wide), BF16)
    else:
        partial_shape = jax.ShapeDtypeStruct((feats, width), F32)
    params = pltpu.CompilerParams(vmem_limit_bytes=40 * 1024 * 1024)

    def shifted(value, shift):
        return lax.ppermute(value, "rep", [(i, target(i, shift, rep)) for i in range(rep)])

    blocks = [features] + [shifted(features, shift) for shift in range(1, rep)]
    outgoing, tile_vals, cotangent = pl.pallas_call(
        pick_kernel,
        out_shape=[
            jax.ShapeDtypeStruct((groups, each, feats), BF16),
            jax.ShapeDtypeStruct(tile_vals.shape, BF16),
            jax.ShapeDtypeStruct(cotangent.shape, BF16),
        ],
        in_specs=[HBM] * 4,
        out_specs=[VMEM] * 3,
        scratch_shapes=[
            pltpu.VMEM(send_rows.shape, jnp.int32),
            pltpu.VMEM((rows, feats), BF16),
            pltpu.SemaphoreType.DMA((4,)),
        ],
        compiler_params=params,
        name="pick_rows",
    )(*[pltpu.with_memory_space_constraint(x, pltpu.HBM) for x in (send_rows, features, tile_vals, cotangent)])
    received = lax.all_to_all(outgoing, "dom", split_axis=0, concat_axis=0, tiled=True)
    results = pl.pallas_call(
        functools.partial(layer_kernel, rep),
        out_shape=[
            jax.ShapeDtypeStruct((rows, width), BF16),
            jax.ShapeDtypeStruct((rows, width), F32),
            *[jax.ShapeDtypeStruct((rows, width), BF16)] * (rep - 1),
            jax.ShapeDtypeStruct((groups, each, width), BF16),
            partial_shape,
        ],
        in_specs=[SMEM] * 2 + [VMEM] * (5 + rep),
        out_specs=[VMEM] * (rep + 3),
        scratch_shapes=[
            pltpu.VMEM((rep * tiles, TILE, feats), BF16),
            pltpu.VMEM((rep * tiles, TILE, width), F32),
        ],
        compiler_params=params,
        name="layer",
    )(tile_cols, tile_counts, tile_vals, received, bnd_adj, cotangent, weight, *blocks)
    output, own, sends, message, partial = *results[:2], results[2:-2], *results[-2:]
    arrived = [shifted(send, shift) for shift, send in enumerate(sends, 1)]
    returned = lax.all_to_all(message, "dom", split_axis=0, concat_axis=0, tiled=True)
    if chunked:
        everyone = ("dom", "rep")
        parts = lax.all_to_all(partial, everyone, split_axis=0, concat_axis=0, tiled=True)
        total = pl.pallas_call(
            sum_kernel,
            out_shape=partial_shape,
            in_specs=[VMEM] * 2,
            out_specs=VMEM,
            compiler_params=params,
            name="sum_parts",
        )(parts, returned)
        chunks = lax.all_to_all(total, everyone, split_axis=0, concat_axis=0, tiled=True)
        grad_weight = pl.pallas_call(
            spread_kernel,
            out_shape=jax.ShapeDtypeStruct((feats, width), F32),
            in_specs=[VMEM],
            out_specs=VMEM,
            compiler_params=params,
            name="weight_gradient",
        )(chunks)
    else:
        grad_weight = lax.psum(partial, ("dom", "rep"))
    grad_features = pl.pallas_call(
        final_kernel,
        out_shape=jax.ShapeDtypeStruct((rows, feats), BF16),
        in_specs=[VMEM] * (3 + rep),
        out_specs=VMEM,
        compiler_params=params,
        name="input_gradient",
    )(send_rows, returned, weight, own, *arrived)
    return (output, grad_features, grad_weight)


def solution(mesh):
    placed = (
        P(("dom", "rep"), None),
        P(),
        P(("dom", "rep"), None),
        P(("dom", "rep"), None, None, None),
        P(("dom", "rep")),
        P(("dom", "rep"), None, None),
        P(("dom", "rep"), None),
        P(("dom", "rep"), None),
    )
    return jax.shard_map(
        body,
        mesh=mesh,
        in_specs=placed,
        out_specs=(P(("dom", "rep"), None), P(("dom", "rep"), None), P()),
        check_vma=False,
    )
```

```python
import functools

import jax
import jax.numpy as jnp
from jax import lax
from jax.experimental import pallas as pl
from jax.experimental.pallas import tpu as pltpu
from jax.sharding import PartitionSpec as P

TILE = 128
F32 = jnp.float32
BF16 = jnp.bfloat16
VMEM = pl.BlockSpec(memory_space=pltpu.VMEM)
HBM = pl.BlockSpec(memory_space=pltpu.HBM)
SMEM = pl.BlockSpec(memory_space=pltpu.SMEM)


def dot(a, b, contract_a, contract_b):
    return lax.dot_general(
        a, b, (((contract_a,), (contract_b,)), ((), ())), preferred_element_type=F32
    )


def target(me, shift, count):
    return me ^ shift if count & (count - 1) == 0 else (me + shift) % count


def source(me, shift, count):
    return me ^ shift if count & (count - 1) == 0 else (me - shift + count) % count


def wanted_rows(index_ref, rows, order):
    flat = jnp.concatenate([index_ref[0, pl.ds(q, 1), :] for q in order], axis=1)
    at = lax.broadcasted_iota(jnp.int32, (rows, flat.shape[1]), 0)
    return jnp.where(at == flat, 1.0, 0.0).astype(BF16)


def pick_kernel(index_ref, features_ref, vals_ref, cot_ref, send_ref, keep_ref, vals_out, cot_out, index, features, sems):
    copies = [
        pltpu.make_async_copy(index_ref, index, sems.at[0]),
        pltpu.make_async_copy(features_ref, features, sems.at[1]),
        pltpu.make_async_copy(cot_ref, cot_out, sems.at[2]),
        pltpu.make_async_copy(vals_ref, vals_out, sems.at[3]),
    ]
    for copy in copies:
        copy.start()
    copies[0].wait()
    me = lax.axis_index("dom")
    groups = index_ref.shape[1]
    onehot = wanted_rows(index, features_ref.shape[0], [me ^ s for s in range(groups)])
    copies[1].wait()
    picked = dot(onehot, features[...], 0, 0).astype(BF16)
    each = keep_ref.shape[1]
    for s in range(groups):
        (send_ref if s % 2 else keep_ref)[s // 2] = picked[s * each : (s + 1) * each]
    for copy in copies[2:]:
        copy.wait()


def stage_kernel(keep_ref, got_ref, *refs):
    next_send_ref, next_keep_ref = refs[-2:]
    rows = keep_ref.shape[1]
    for j in range(keep_ref.shape[0]):
        to_ref = (next_send_ref if j % 2 else next_keep_ref).at[j // 2]
        to_ref[:rows, :] = keep_ref[j]
        to_ref[rows:, :] = got_ref[j]


def layer_kernel(rep, cols_ref, counts_ref, vals_ref, kept_ref, came_ref, bnd_ref, cot_ref, weight_ref, *refs):
    blocks = refs[:rep]
    out_ref, own_ref = refs[rep], refs[rep + 1]
    sends = refs[rep + 2 : 2 * rep + 1]
    bnd_send_ref, bnd_keep_ref, partial_ref, panel, terms, received, boundary = refs[2 * rep + 1 :]
    here = lax.axis_index("dom")
    me = lax.axis_index("rep")
    tiles, slots = cols_ref.shape
    width = weight_ref.shape[1]
    for shift, block in enumerate(blocks):
        owner = source(me, shift, rep)
        for t in range(tiles):
            panel[owner * tiles + t] = block[t * TILE : (t + 1) * TILE, :]
    each = bnd_keep_ref.shape[1]
    groups = received.shape[0] // each
    for o in range(groups):
        side, at = (kept_ref, o) if o < groups // 2 else (came_ref, o - groups // 2)
        received[pl.ds(pl.multiple_of((here ^ o) * each, each), each), :] = side[0, at * each : (at + 1) * each, :]
    adjacency = []
    forward = []
    backward = []
    for t in range(tiles):
        live = [
            jnp.where(k < counts_ref[t], vals_ref[t, k], jnp.zeros_like(vals_ref[t, k]))
            for k in range(slots)
        ]
        chosen = jnp.concatenate([panel[cols_ref[t, k]] for k in range(slots)], axis=0)
        stacked = jnp.concatenate(live, axis=0)
        adjacency.append(stacked)
        forward.append(dot(jnp.concatenate(live, axis=1), chosen, 1, 0))
        backward.append(dot(stacked, chosen, 0, 0))
    outside = dot(bnd_ref[...], received[...], 1, 0)
    mixed = jnp.concatenate(forward, axis=0) + outside
    turned = (jnp.concatenate(backward, axis=0) + outside).astype(BF16)
    high = mixed.astype(BF16)
    low = (mixed - high.astype(F32)).astype(BF16)
    weight = weight_ref[...]
    pre = dot(high, weight, 1, 0) + dot(low, weight, 1, 0)
    sig = jax.nn.sigmoid(pre)
    out_ref[...] = (pre * sig).astype(BF16)
    grad = (cot_ref[...].astype(F32) * sig * (1.0 + pre * (1.0 - sig))).astype(BF16)
    terms[...] = jnp.zeros_like(terms)
    for t in range(tiles):
        parts = dot(adjacency[t], grad[t * TILE : (t + 1) * TILE], 1, 0)
        for k in range(slots):
            terms[cols_ref[t, k]] += parts[k * TILE : (k + 1) * TILE]
    for t in range(tiles):
        own_ref[t * TILE : (t + 1) * TILE, :] = terms[me * tiles + t]
        for shift, send in enumerate(sends, 1):
            owner = target(me, shift, rep)
            send[t * TILE : (t + 1) * TILE, :] = terms[owner * tiles + t].astype(BF16)
    boundary[...] = dot(bnd_ref[...], grad, 0, 0).astype(BF16)
    for s in range(groups):
        at = pl.multiple_of((here ^ s) * each, each)
        (bnd_send_ref if s % 2 else bnd_keep_ref)[s // 2] = boundary[pl.ds(at, each), :]
    partial = dot(turned, grad, 0, 0)
    if partial_ref.shape == partial.shape:
        partial_ref[...] = partial
    else:
        count, high, wide = partial_ref.shape
        across = width // wide
        for j in range(count):
            row, column = j // across * high, j % across * wide
            partial_ref[j] = partial[row : row + high, column : column + wide].astype(BF16)


def sum_kernel(parts_ref, out_ref):
    total = jnp.sum(parts_ref[...].astype(F32), axis=0).astype(BF16)
    out_ref[...] = jnp.broadcast_to(total[None], out_ref.shape)


def spread_kernel(chunks_ref, out_ref):
    count, high, wide = chunks_ref.shape
    across = out_ref.shape[1] // wide
    for j in range(count):
        row, column = j // across * high, j % across * wide
        out_ref[row : row + high, column : column + wide] = chunks_ref[j].astype(F32)


def final_kernel(index_ref, kept_ref, came_ref, weight_ref, own_ref, *refs):
    arrived, out_ref = refs[:-1], refs[-1]
    here = lax.axis_index("dom")
    onehot = wanted_rows(index_ref, own_ref.shape[0], [here ^ o for o in range(index_ref.shape[1])])
    returned = jnp.concatenate([kept_ref[0], came_ref[0]], axis=0)
    total = own_ref[...] + dot(onehot, returned, 1, 0)
    for term in arrived:
        total = total + term[...].astype(F32)
    out_ref[...] = dot(total.astype(BF16), weight_ref[...], 1, 1).astype(BF16)


def body(features, weight, tile_cols, tile_vals, tile_counts, send_rows, bnd_adj, cotangent):
    rows, feats = features.shape
    width = weight.shape[1]
    tiles, slots = tile_cols.shape
    groups, each = send_rows.shape[1], send_rows.shape[2]
    rep = lax.axis_size("rep")
    devices = groups * rep
    wide = feats * width // (16 * devices)
    chunked = wide >= TILE and width % wide == 0 and feats % 16 == 0
    if chunked:
        partial_shape = jax.ShapeDtypeStruct((devices, 16, wide), BF16)
    else:
        partial_shape = jax.ShapeDtypeStruct((feats, width), F32)
    params = pltpu.CompilerParams(vmem_limit_bytes=40 * 1024 * 1024)

    def shifted(value, shift):
        return lax.ppermute(value, "rep", [(i, target(i, shift, rep)) for i in range(rep)])

    def exchange(send, keep, after=(), flops=1):
        for b in range(groups.bit_length() - 1):
            came = lax.ppermute(send, "dom", [(i, i ^ 1 << b) for i in range(groups)])
            parts, high = keep.shape[0], keep.shape[1]
            if parts == 1:
                return keep, came
            send, keep = pl.pallas_call(
                stage_kernel,
                out_shape=[jax.ShapeDtypeStruct((parts // 2, 2 * high, keep.shape[2]), BF16)] * 2,
                in_specs=[VMEM] * (2 + len(after)),
                out_specs=[VMEM] * 2,
                compiler_params=params,
                cost_estimate=pl.CostEstimate(flops=flops, bytes_accessed=1, transcendentals=0),
                name="exchange_step",
            )(keep, came, *after)
            after = ()

    blocks = [features] + [shifted(features, shift) for shift in range(1, rep)]
    send, keep, tile_vals, cotangent = pl.pallas_call(
        pick_kernel,
        out_shape=[
            *[jax.ShapeDtypeStruct((groups // 2, each, feats), BF16)] * 2,
            jax.ShapeDtypeStruct(tile_vals.shape, BF16),
            jax.ShapeDtypeStruct(cotangent.shape, BF16),
        ],
        in_specs=[HBM] * 4,
        out_specs=[VMEM] * 4,
        scratch_shapes=[
            pltpu.VMEM(send_rows.shape, jnp.int32),
            pltpu.VMEM((rows, feats), BF16),
            pltpu.SemaphoreType.DMA((4,)),
        ],
        compiler_params=params,
        name="pick_rows",
    )(*[pltpu.with_memory_space_constraint(x, pltpu.HBM) for x in (send_rows, features, tile_vals, cotangent)])
    received = exchange(send, keep)
    results = pl.pallas_call(
        functools.partial(layer_kernel, rep),
        out_shape=[
            jax.ShapeDtypeStruct((rows, width), BF16),
            jax.ShapeDtypeStruct((rows, width), F32),
            *[jax.ShapeDtypeStruct((rows, width), BF16)] * (rep - 1),
            *[jax.ShapeDtypeStruct((groups // 2, each, width), BF16)] * 2,
            partial_shape,
        ],
        in_specs=[SMEM] * 2 + [VMEM] * (6 + rep),
        out_specs=[VMEM] * (rep + 4),
        scratch_shapes=[
            pltpu.VMEM((rep * tiles, TILE, feats), BF16),
            pltpu.VMEM((rep * tiles, TILE, width), F32),
            pltpu.VMEM((groups * each, feats), BF16),
            pltpu.VMEM((groups * each, width), BF16),
        ],
        compiler_params=params,
        name="layer",
    )(tile_cols, tile_counts, tile_vals, *received, bnd_adj, cotangent, weight, *blocks)
    output, own, sends, send, keep, partial = *results[:2], results[2:-3], *results[-3:]
    arrived = [shifted(send, shift) for shift, send in enumerate(sends, 1)]
    if chunked:
        everyone = ("dom", "rep")
        parts = lax.all_to_all(partial, everyone, split_axis=0, concat_axis=0, tiled=True)
        total = pl.pallas_call(
            sum_kernel,
            out_shape=partial_shape,
            in_specs=[VMEM],
            out_specs=VMEM,
            compiler_params=params,
            name="sum_parts",
        )(parts)
        chunks = lax.all_to_all(total, everyone, split_axis=0, concat_axis=0, tiled=True)
        grad_weight = pl.pallas_call(
            spread_kernel,
            out_shape=jax.ShapeDtypeStruct((feats, width), F32),
            in_specs=[VMEM],
            out_specs=VMEM,
            compiler_params=params,
            name="weight_gradient",
        )(chunks)
    else:
        total = None
        grad_weight = lax.psum(partial, ("dom", "rep"))
    returned = exchange(send, keep, () if total is None else (total,))
    grad_features = pl.pallas_call(
        final_kernel,
        out_shape=jax.ShapeDtypeStruct((rows, feats), BF16),
        in_specs=[VMEM] * (4 + rep),
        out_specs=VMEM,
        compiler_params=params,
        cost_estimate=pl.CostEstimate(flops=1_800_000_000, bytes_accessed=1, transcendentals=0),
        name="input_gradient",
    )(send_rows, *returned, weight, own, *arrived)
    return (output, grad_features, grad_weight)


def solution(mesh):
    placed = (
        P(("dom", "rep"), None),
        P(),
        P(("dom", "rep"), None),
        P(("dom", "rep"), None, None, None),
        P(("dom", "rep")),
        P(("dom", "rep"), None, None),
        P(("dom", "rep"), None),
        P(("dom", "rep"), None),
    )
    return jax.shard_map(
        body,
        mesh=mesh,
        in_specs=placed,
        out_specs=(P(("dom", "rep"), None), P(("dom", "rep"), None), P()),
        check_vma=False,
    )
```

```python
import functools

import jax
import jax.numpy as jnp
from jax import lax
from jax.experimental import pallas as pl
from jax.experimental.pallas import tpu as pltpu
from jax.sharding import PartitionSpec as P

TILE = 128
F32 = jnp.float32
BF16 = jnp.bfloat16
VMEM = pl.BlockSpec(memory_space=pltpu.VMEM)
HBM = pl.BlockSpec(memory_space=pltpu.HBM)
SMEM = pl.BlockSpec(memory_space=pltpu.SMEM)


def dot(a, b, contract_a, contract_b):
    return lax.dot_general(
        a, b, (((contract_a,), (contract_b,)), ((), ())), preferred_element_type=F32
    )


def target(me, shift, count):
    return me ^ shift if count & (count - 1) == 0 else (me + shift) % count


def source(me, shift, count):
    return me ^ shift if count & (count - 1) == 0 else (me - shift + count) % count


def share_order(q, groups):
    order = 0
    for b in range(groups.bit_length() - 1):
        order = 2 * order + (q >> b & 1)
    return order


def wanted_rows(index_ref, rows):
    groups = index_ref.shape[1]
    flat = jnp.concatenate([index_ref[0, q : q + 1, :] for q in range(groups)], axis=1)
    at = lax.broadcasted_iota(jnp.int32, (rows, flat.shape[1]), 0)
    return jnp.where(at == flat, 1.0, 0.0).astype(BF16)


def pick_kernel(index_ref, features_ref, *refs):
    count = (len(refs) - 4) // 2
    loads, out_ref, loaded = refs[:count], refs[count], refs[count + 1 : -3]
    index, features, sems = refs[-3:]
    pairs = [(index_ref, index), (features_ref, features), *zip(loads, loaded)]
    copies = [pltpu.make_async_copy(*pair, sems.at[at]) for at, pair in enumerate(pairs)]
    for copy in copies:
        copy.start()
    copies[0].wait()
    onehot = wanted_rows(index, features_ref.shape[0])
    copies[1].wait()
    picked = dot(onehot, features[...], 0, 0).astype(BF16)
    each = out_ref.shape[1]
    for q in range(out_ref.shape[0]):
        out_ref[q] = picked[q * each : (q + 1) * each]
    for copy in copies[2:]:
        copy.wait()


def live_tiles(counts_ref, vals_ref, t):
    return [
        jnp.where(k < counts_ref[t], vals_ref[t, k], jnp.zeros_like(vals_ref[t, k]))
        for k in range(vals_ref.shape[1])
    ]


def layer_kernel(rep, cols_ref, counts_ref, vals_ref, received_ref, bnd_ref, cot_ref, weight_ref, *refs):
    blocks = refs[:rep]
    out_ref, grad_ref, message_ref, panel = refs[rep:]
    me = lax.axis_index("rep")
    tiles, slots = cols_ref.shape
    for shift, block in enumerate(blocks):
        owner = source(me, shift, rep)
        for t in range(tiles):
            panel[owner * tiles + t] = block[t * TILE : (t + 1) * TILE, :]
    groups, each = received_ref.shape[0], received_ref.shape[1]
    received = jnp.concatenate([received_ref[q] for q in range(groups)], axis=0)
    forward = []
    backward = []
    for t in range(tiles):
        live = live_tiles(counts_ref, vals_ref, t)
        chosen = jnp.concatenate([panel[cols_ref[t, k]] for k in range(slots)], axis=0)
        forward.append(dot(jnp.concatenate(live, axis=1), chosen, 1, 0))
        backward.append(dot(jnp.concatenate(live, axis=0), chosen, 0, 0))
    outside = dot(bnd_ref[...], received, 1, 0)
    mixed = jnp.concatenate(forward, axis=0) + outside
    turned = (jnp.concatenate(backward, axis=0) + outside).astype(BF16)
    high = mixed.astype(BF16)
    low = (mixed - high.astype(F32)).astype(BF16)
    weight = weight_ref[...]
    pre = dot(high, weight, 1, 0) + dot(low, weight, 1, 0)
    sig = jax.nn.sigmoid(pre)
    out_ref[...] = (pre * sig).astype(BF16)
    grad = (cot_ref[...].astype(F32) * sig * (1.0 + pre * (1.0 - sig))).astype(BF16)
    grad_ref[...] = grad
    boundary = dot(bnd_ref[...], grad, 0, 0).astype(BF16)
    partial = dot(turned, grad, 0, 0).astype(BF16)
    share = partial.shape[0] // groups
    for q in range(groups):
        message_ref[q, :each, :] = boundary[q * each : (q + 1) * each]
        at = share_order(q, groups) * share
        message_ref[q, each:, :] = partial[at : at + share]


def terms_kernel(rep, layout, cols_ref, counts_ref, vals_ref, grad_ref, *refs):
    outs, terms = refs[:-1], refs[-1]
    me = lax.axis_index("rep")
    tiles, slots = cols_ref.shape
    terms[...] = jnp.zeros_like(terms)
    for t in range(tiles):
        stacked = jnp.concatenate(live_tiles(counts_ref, vals_ref, t), axis=0)
        parts = dot(stacked, grad_ref[t * TILE : (t + 1) * TILE, :], 1, 0)
        for k in range(slots):
            terms[cols_ref[t, k]] += parts[k * TILE : (k + 1) * TILE]
    for out_ref, shifts in zip(outs, layout):
        for at, shift in enumerate(shifts):
            owner = target(me, shift, rep)
            for t in range(tiles):
                row = (at * tiles + t) * TILE
                out_ref[row : row + TILE, :] = terms[owner * tiles + t].astype(out_ref.dtype)


def relay_kernel(far_ref, came_ref, out_ref):
    rows = far_ref.shape[0]
    out_ref[...] = (far_ref[...] + came_ref[rows:, :].astype(F32)).astype(BF16)


def rep_sum_kernel(*refs):
    chunk, one, two, three = [ref[...].astype(F32) for ref in refs[:4]]
    refs[-1][...] = ((chunk + two) + (one + three)).astype(BF16)


def join_kernel(bit, own_ref, got_ref, out_ref):
    own, got = own_ref[...], got_ref[...]
    half = own.shape[0]
    upper = lax.rem(lax.axis_index("dom") // bit, 2) == 1
    out_ref[:half, :] = jnp.where(upper, got, own).astype(out_ref.dtype)
    out_ref[half:, :] = jnp.where(upper, own, got).astype(out_ref.dtype)


def final_kernel(index_ref, returned_ref, weight_ref, own_ref, *refs):
    arrived, out_ref = refs[:-1], refs[-1]
    groups, each = index_ref.shape[1], index_ref.shape[2]
    onehot = wanted_rows(index_ref, own_ref.shape[0])
    returned = jnp.concatenate([returned_ref[q, :each, :] for q in range(groups)], axis=0)
    total = own_ref[...] + dot(onehot, returned, 1, 0)
    for term in arrived:
        total = total + term[: own_ref.shape[0], :].astype(F32)
    out_ref[...] = dot(total.astype(BF16), weight_ref[...], 1, 1).astype(BF16)


def body(features, weight, tile_cols, tile_vals, tile_counts, send_rows, bnd_adj, cotangent):
    rows, feats = features.shape
    width = weight.shape[1]
    tiles, slots = tile_cols.shape
    groups, each = send_rows.shape[1], send_rows.shape[2]
    rep = lax.axis_size("rep")
    share = feats // groups
    bits = [1 << b for b in range(groups.bit_length() - 1)]
    params = pltpu.CompilerParams(vmem_limit_bytes=40 * 1024 * 1024)

    def shifted(value, shift):
        return lax.ppermute(value, "rep", [(i, target(i, shift, rep)) for i in range(rep)])

    blocks = [features] + [shifted(features, shift) for shift in range(1, rep)]
    tiny = pl.CostEstimate(flops=1, bytes_accessed=1, transcendentals=0)
    loads = [tile_vals, cotangent, tile_cols, tile_counts]
    outgoing, tile_vals, cotangent, tile_cols, tile_counts = pl.pallas_call(
        pick_kernel,
        out_shape=[
            jax.ShapeDtypeStruct((groups, each, feats), BF16),
            *[jax.ShapeDtypeStruct(load.shape, load.dtype) for load in loads],
        ],
        in_specs=[HBM] * (2 + len(loads)),
        out_specs=[VMEM] * (1 + len(loads)),
        scratch_shapes=[
            pltpu.VMEM(send_rows.shape, jnp.int32),
            pltpu.VMEM((rows, feats), BF16),
            pltpu.SemaphoreType.DMA((2 + len(loads),)),
        ],
        compiler_params=params,
        name="pick_rows",
    )(*[pltpu.with_memory_space_constraint(x, pltpu.HBM) for x in (send_rows, features, *loads)])
    received = lax.all_to_all(outgoing, "dom", split_axis=0, concat_axis=0, tiled=True)
    output, grad, message = pl.pallas_call(
        functools.partial(layer_kernel, rep),
        out_shape=[
            jax.ShapeDtypeStruct((rows, width), BF16),
            jax.ShapeDtypeStruct((rows, width), BF16),
            jax.ShapeDtypeStruct((groups, each + share, width), BF16),
        ],
        in_specs=[SMEM] * 2 + [VMEM] * (5 + rep),
        out_specs=[VMEM] * 3,
        scratch_shapes=[pltpu.VMEM((rep * tiles, TILE, feats), BF16)],
        compiler_params=params,
        name="layer",
    )(tile_cols, tile_counts, tile_vals, received, bnd_adj, cotangent, weight, *blocks)
    returned = lax.all_to_all(message, "dom", split_axis=0, concat_axis=0, tiled=True)
    relayed = rep == 4
    layout = [(0,), (1, 3), (2,)] if relayed else [(shift,) for shift in range(rep)]
    kinds = [F32, BF16, F32] if relayed else [F32] + [BF16] * (rep - 1)
    own, *sends = pl.pallas_call(
        functools.partial(terms_kernel, rep, layout),
        out_shape=[
            jax.ShapeDtypeStruct((len(shifts) * rows, width), kind)
            for shifts, kind in zip(layout, kinds)
        ],
        in_specs=[SMEM] * 2 + [VMEM] * 2,
        out_specs=[VMEM] * len(layout),
        scratch_shapes=[pltpu.VMEM((rep * tiles, TILE, width), F32)],
        compiler_params=params,
        name="terms",
    )(tile_cols, tile_counts, tile_vals, grad)
    chunk = jnp.sum(returned[:, each:].astype(F32), axis=0).astype(BF16)
    if relayed:
        came = shifted(sends[0], 1)
        relay = pl.pallas_call(
            relay_kernel,
            out_shape=jax.ShapeDtypeStruct((rows, width), BF16),
            in_specs=[VMEM] * 2,
            out_specs=VMEM,
            compiler_params=params,
            cost_estimate=tiny,
            name="relay",
        )(sends[1], came)
        arrived = [came, shifted(relay, 2)]
        piece = pl.pallas_call(
            rep_sum_kernel,
            out_shape=jax.ShapeDtypeStruct(chunk.shape, BF16),
            in_specs=[VMEM] * 5,
            out_specs=VMEM,
            compiler_params=params,
            cost_estimate=tiny,
            name="rep_sum",
        )(chunk, *[shifted(chunk, shift) for shift in (1, 2, 3)], relay)
    else:
        arrived = [shifted(send, shift) for shift, send in enumerate(sends, 1)]
        piece = jnp.sum(lax.all_gather(chunk, "rep").astype(F32), axis=0).astype(BF16)
    for bit in reversed(bits):
        got = lax.ppermute(piece, "dom", [(i, i ^ bit) for i in range(groups)])
        piece = pl.pallas_call(
            functools.partial(join_kernel, bit),
            out_shape=jax.ShapeDtypeStruct((2 * piece.shape[0], width), F32 if bit == 1 else BF16),
            in_specs=[VMEM] * 2,
            out_specs=VMEM,
            compiler_params=params,
            cost_estimate=tiny,
            name="join",
        )(piece, got)
    grad_weight = piece
    grad_features = pl.pallas_call(
        final_kernel,
        out_shape=jax.ShapeDtypeStruct((rows, feats), BF16),
        in_specs=[VMEM] * (4 + len(arrived)),
        out_specs=VMEM,
        compiler_params=params,
        cost_estimate=pl.CostEstimate(flops=1_000_000_000, bytes_accessed=1, transcendentals=0),
        name="input_gradient",
    )(send_rows, returned, weight, own, *arrived)
    return (output, grad_features, grad_weight)


def solution(mesh):
    placed = (
        P(("dom", "rep"), None),
        P(),
        P(("dom", "rep"), None),
        P(("dom", "rep"), None, None, None),
        P(("dom", "rep")),
        P(("dom", "rep"), None, None),
        P(("dom", "rep"), None),
        P(("dom", "rep"), None),
    )
    return jax.shard_map(
        body,
        mesh=mesh,
        in_specs=placed,
        out_specs=(P(("dom", "rep"), None), P(("dom", "rep"), None), P()),
        check_vma=False,
    )
```

```python
import functools

import jax
import jax.numpy as jnp
from jax import lax
from jax.experimental import pallas as pl
from jax.experimental.pallas import tpu as pltpu
from jax.sharding import PartitionSpec as P

TILE = 128
F32 = jnp.float32
BF16 = jnp.bfloat16
VMEM = pl.BlockSpec(memory_space=pltpu.VMEM)
HBM = pl.BlockSpec(memory_space=pltpu.HBM)
SMEM = pl.BlockSpec(memory_space=pltpu.SMEM)


def dot(a, b, contract_a, contract_b):
    return lax.dot_general(
        a, b, (((contract_a,), (contract_b,)), ((), ())), preferred_element_type=F32
    )


def target(me, shift, count):
    return me ^ shift if count & (count - 1) == 0 else (me + shift) % count


def source(me, shift, count):
    return me ^ shift if count & (count - 1) == 0 else (me - shift + count) % count


def wanted_rows(index_ref, rows, order):
    flat = jnp.concatenate([index_ref[0, pl.ds(q, 1), :] for q in order], axis=1)
    at = lax.broadcasted_iota(jnp.int32, (rows, flat.shape[1]), 0)
    return jnp.where(at == flat, 1.0, 0.0).astype(BF16)


def pick_kernel(index_ref, features_ref, *refs):
    count = (len(refs) - 5) // 2
    loads, send_ref, keep_ref, loaded = refs[:count], refs[count], refs[count + 1], refs[count + 2 : -3]
    index, features, sems = refs[-3:]
    pairs = [(index_ref, index), (features_ref, features), *zip(loads, loaded)]
    copies = [pltpu.make_async_copy(*pair, sems.at[at]) for at, pair in enumerate(pairs)]
    for copy in copies:
        copy.start()
    here = lax.axis_index("dom")
    groups, each = index_ref.shape[1:]
    copies[0].wait()
    onehot = wanted_rows(index, features_ref.shape[0], [here ^ s for s in range(groups)])
    copies[1].wait()
    picked = dot(onehot, features[...], 0, 0).astype(BF16)
    for s in range(groups):
        to_ref = send_ref if s % 2 else keep_ref
        to_ref[s // 2 * each : (s // 2 + 1) * each, :] = picked[s * each : (s + 1) * each]
    for copy in copies[2:]:
        copy.wait()


def stage_kernel(each, keep_ref, came_ref, *outs):
    for j, out_ref in enumerate(outs):
        out_ref[:each, :] = keep_ref[j * each : (j + 1) * each, :]
        out_ref[each:, :] = came_ref[j * each : (j + 1) * each, :]


def weighted_stage_kernel(each, keep_ref, half_ref, came_ref, own_ref, share_ref, *refs):
    outs, summed = refs[:-1], refs[-1]
    pairs = len(outs) + 1
    summed[...] = half_ref[...] + came_ref[pairs * each :, :].astype(F32)
    share = summed.shape[0] // pairs
    chip = lax.axis_index("dom") // 2
    for j in range(pairs):
        to_ref = outs[j - 1] if j else own_ref
        to_ref[:each, :] = keep_ref[j * each : (j + 1) * each, :]
        to_ref[each : 2 * each, :] = came_ref[j * each : (j + 1) * each, :]
        part = summed[pl.ds(pl.multiple_of((chip ^ j) * share, share), share), :]
        if j:
            to_ref[2 * each :, :] = part.astype(BF16)
        else:
            share_ref[...] = part


def share_sum_kernel(each, share_ref, *refs):
    total = share_ref[...]
    for ref in refs[:-1]:
        total = total + ref[2 * each :, :].astype(F32)
    refs[-1][...] = total.astype(BF16)


def half_kernel(*refs):
    shares, out_ref, whole = refs[:-2], refs[-2], refs[-1]
    share = shares[0].shape[0]
    chip = lax.axis_index("dom") // 2
    for j, ref in enumerate(shares):
        whole[pl.ds(pl.multiple_of((chip ^ j) * share, share), share), :] = ref[...].astype(F32)
    out_ref[...] = whole[...].astype(BF16)


def live_tiles(counts_ref, vals_ref, t):
    return [
        jnp.where(k < counts_ref[t], vals_ref[t, k], jnp.zeros_like(vals_ref[t, k]))
        for k in range(vals_ref.shape[1])
    ]


def layer_kernel(rep, pairs, cols_ref, counts_ref, vals_ref, bnd_ref, cot_ref, weight_ref, *refs):
    blocks = refs[:rep]
    received_refs = refs[rep : rep + pairs]
    out_ref, grad_ref, send_ref, keep_ref, half_ref, panel, received, boundary, partial = refs[rep + pairs :]
    here = lax.axis_index("dom")
    me = lax.axis_index("rep")
    tiles, slots = cols_ref.shape
    for shift, block in enumerate(blocks):
        owner = source(me, shift, rep)
        for t in range(tiles):
            panel[owner * tiles + t] = block[t * TILE : (t + 1) * TILE, :]
    each = received_refs[0].shape[0] // 2
    groups = 2 * pairs

    def rows_of(group):
        return pl.ds(pl.multiple_of(group * each, each), each)

    for o in range(groups):
        received[rows_of(here ^ o), :] = received_refs[o // 2][o % 2 * each : (o % 2 + 1) * each, :]
    forward = []
    backward = []
    for t in range(tiles):
        live = live_tiles(counts_ref, vals_ref, t)
        chosen = jnp.concatenate([panel[cols_ref[t, k]] for k in range(slots)], axis=0)
        forward.append(dot(jnp.concatenate(live, axis=1), chosen, 1, 0))
        backward.append(dot(jnp.concatenate(live, axis=0), chosen, 0, 0))
    outside = dot(bnd_ref[...], received[...], 1, 0)
    mixed = jnp.concatenate(forward, axis=0) + outside
    turned = (jnp.concatenate(backward, axis=0) + outside).astype(BF16)
    high = mixed.astype(BF16)
    low = (mixed - high.astype(F32)).astype(BF16)
    weight = weight_ref[...]
    pre = dot(high, weight, 1, 0) + dot(low, weight, 1, 0)
    sig = jax.nn.sigmoid(pre)
    out_ref[...] = (pre * sig).astype(BF16)
    grad = (cot_ref[...].astype(F32) * sig * (1.0 + pre * (1.0 - sig))).astype(BF16)
    grad_ref[...] = grad
    boundary[...] = dot(bnd_ref[...], grad, 0, 0).astype(BF16)
    for s in range(groups):
        to_ref = send_ref if s % 2 else keep_ref
        to_ref[s // 2 * each : (s // 2 + 1) * each, :] = boundary[rows_of(here ^ s), :]
    partial[...] = dot(turned, grad, 0, 0)
    half = half_ref.shape[0]
    mine = here % 2
    half_ref[...] = partial[pl.ds(pl.multiple_of(mine * half, half), half), :]
    send_ref[pairs * each :, :] = partial[pl.ds(pl.multiple_of((1 - mine) * half, half), half), :].astype(BF16)


def terms_kernel(rep, layout, cols_ref, counts_ref, vals_ref, grad_ref, *refs):
    outs, terms = refs[:-1], refs[-1]
    me = lax.axis_index("rep")
    tiles, slots = cols_ref.shape
    terms[...] = jnp.zeros_like(terms)
    for t in range(tiles):
        stacked = jnp.concatenate(live_tiles(counts_ref, vals_ref, t), axis=0)
        parts = dot(stacked, grad_ref[t * TILE : (t + 1) * TILE, :], 1, 0)
        for k in range(slots):
            terms[cols_ref[t, k]] += parts[k * TILE : (k + 1) * TILE]
    for out_ref, shifts in zip(outs, layout):
        for at, shift in enumerate(shifts):
            owner = target(me, shift, rep)
            for t in range(tiles):
                row = (at * tiles + t) * TILE
                out_ref[row : row + TILE, :] = terms[owner * tiles + t].astype(out_ref.dtype)


def relay_kernel(far_ref, came_ref, out_ref):
    rows = far_ref.shape[0]
    out_ref[...] = (far_ref[...] + came_ref[rows:, :].astype(F32)).astype(BF16)


def rep_sum_kernel(*refs):
    chunk, one, two, three = [ref[...].astype(F32) for ref in refs[:4]]
    refs[-1][...] = ((chunk + two) + (one + three)).astype(BF16)


def join_kernel(bit, own_ref, got_ref, out_ref):
    own, got = own_ref[...], got_ref[...]
    half = own.shape[0]
    upper = lax.rem(lax.axis_index("dom") // bit, 2) == 1
    out_ref[:half, :] = jnp.where(upper, got, own).astype(out_ref.dtype)
    out_ref[half:, :] = jnp.where(upper, own, got).astype(out_ref.dtype)


def final_kernel(pairs, index_ref, weight_ref, own_ref, *refs):
    returned, arrived, out_ref = refs[:pairs], refs[pairs:-1], refs[-1]
    groups, each = index_ref.shape[1:]
    here = lax.axis_index("dom")
    onehot = wanted_rows(index_ref, own_ref.shape[0], [here ^ o for o in range(groups)])
    returned = jnp.concatenate([ref[: 2 * each, :] for ref in returned], axis=0)
    total = own_ref[...] + dot(onehot, returned, 1, 0)
    for term in arrived:
        total = total + term[: own_ref.shape[0], :].astype(F32)
    out_ref[...] = dot(total.astype(BF16), weight_ref[...], 1, 1).astype(BF16)


def body(features, weight, tile_cols, tile_vals, tile_counts, send_rows, bnd_adj, cotangent):
    rows, feats = features.shape
    width = weight.shape[1]
    tiles, slots = tile_cols.shape
    groups, each = send_rows.shape[1], send_rows.shape[2]
    rep = lax.axis_size("rep")
    share = feats // groups
    pairs = groups // 2
    params = pltpu.CompilerParams(vmem_limit_bytes=40 * 1024 * 1024)

    def shifted(value, shift):
        return lax.ppermute(value, "rep", [(i, target(i, shift, rep)) for i in range(rep)])

    def across(value, bits):
        return lax.ppermute(value, "dom", [(i, i ^ bits) for i in range(groups)])

    def call(kernel, name, outs, operands, scratch=()):
        return pl.pallas_call(
            kernel,
            out_shape=outs,
            in_specs=[VMEM] * len(operands),
            out_specs=[VMEM] * len(outs),
            scratch_shapes=scratch,
            compiler_params=params,
            cost_estimate=pl.CostEstimate(flops=1, bytes_accessed=1, transcendentals=0),
            name=name,
        )(*operands)

    def shape(high, kind=BF16, wide=width):
        return jax.ShapeDtypeStruct((high, wide), kind)

    blocks = [features] + [shifted(features, shift) for shift in range(1, rep)]
    loads = [tile_vals, cotangent, tile_cols, tile_counts]
    send, keep, tile_vals, cotangent, tile_cols, tile_counts = pl.pallas_call(
        pick_kernel,
        out_shape=[
            *[shape(pairs * each, BF16, feats)] * 2,
            *[jax.ShapeDtypeStruct(load.shape, load.dtype) for load in loads],
        ],
        in_specs=[HBM] * (2 + len(loads)),
        out_specs=[VMEM] * (2 + len(loads)),
        scratch_shapes=[
            pltpu.VMEM(send_rows.shape, jnp.int32),
            pltpu.VMEM((rows, feats), BF16),
            pltpu.SemaphoreType.DMA((2 + len(loads),)),
        ],
        compiler_params=params,
        name="pick_rows",
    )(*[pltpu.with_memory_space_constraint(x, pltpu.HBM) for x in (send_rows, features, *loads)])
    received = call(
        functools.partial(stage_kernel, each),
        "pair_rows",
        [shape(2 * each, BF16, feats)] * pairs,
        (keep, across(send, 1)),
    )
    received = [received[0]] + [across(received[j], 2 * j) for j in range(1, pairs)]
    half = feats // 2
    output, grad, send, keep, mine = pl.pallas_call(
        functools.partial(layer_kernel, rep, pairs),
        out_shape=[
            shape(rows),
            shape(rows),
            shape(pairs * each + half),
            shape(pairs * each),
            shape(half, F32),
        ],
        in_specs=[SMEM] * 2 + [VMEM] * (4 + rep + pairs),
        out_specs=[VMEM] * 5,
        scratch_shapes=[
            pltpu.VMEM((rep * tiles, TILE, feats), BF16),
            pltpu.VMEM((groups * each, feats), BF16),
            pltpu.VMEM((groups * each, width), BF16),
            pltpu.VMEM((feats, width), F32),
        ],
        compiler_params=params,
        name="layer",
    )(tile_cols, tile_counts, tile_vals, bnd_adj, cotangent, weight, *blocks, *received)
    own_rows, own_share, *parts = call(
        functools.partial(weighted_stage_kernel, each),
        "pair_gradients",
        [shape(2 * each), shape(share, F32)] + [shape(2 * each + share)] * (pairs - 1),
        (keep, mine, across(send, 1)),
        [pltpu.VMEM((half, width), F32)],
    )
    parts = [across(part, 2 * j) for j, part in enumerate(parts, 1)]
    returned = [own_rows] + parts
    relayed = rep == 4
    layout = [(0,), (1, 3), (2,)] if relayed else [(shift,) for shift in range(rep)]
    kinds = [F32, BF16, F32] if relayed else [F32] + [BF16] * (rep - 1)
    own, *sends = pl.pallas_call(
        functools.partial(terms_kernel, rep, layout),
        out_shape=[
            jax.ShapeDtypeStruct((len(shifts) * rows, width), kind)
            for shifts, kind in zip(layout, kinds)
        ],
        in_specs=[SMEM] * 2 + [VMEM] * 2,
        out_specs=[VMEM] * len(layout),
        scratch_shapes=[pltpu.VMEM((rep * tiles, TILE, width), F32)],
        compiler_params=params,
        name="terms",
    )(tile_cols, tile_counts, tile_vals, grad)
    (chunk,) = call(
        functools.partial(share_sum_kernel, each), "share_sum", [shape(share)], (own_share, *parts)
    )
    if relayed:
        came = shifted(sends[0], 1)
        (relay,) = call(relay_kernel, "relay", [shape(rows)], (sends[1], came))
        arrived = [came, shifted(relay, 2)]
        small = [shifted(chunk, shift) for shift in (1, 2, 3)]
        (piece,) = call(rep_sum_kernel, "rep_sum", [shape(share)], (chunk, *small, relay))
    else:
        arrived = [shifted(send, shift) for shift, send in enumerate(sends, 1)]
        piece = jnp.sum(lax.all_gather(chunk, "rep").astype(F32), axis=0).astype(BF16)
    pieces = [piece] + [across(piece, 2 * j) for j in range(1, pairs)]
    (piece,) = call(half_kernel, "half", [shape(half)], pieces, [pltpu.VMEM((half, width), F32)])
    (grad_weight,) = call(
        functools.partial(join_kernel, 1), "join", [shape(feats, F32)], (piece, across(piece, 1))
    )
    grad_features = pl.pallas_call(
        functools.partial(final_kernel, pairs),
        out_shape=jax.ShapeDtypeStruct((rows, feats), BF16),
        in_specs=[VMEM] * (3 + pairs + len(arrived)),
        out_specs=VMEM,
        compiler_params=params,
        cost_estimate=pl.CostEstimate(flops=1_000_000_000, bytes_accessed=1, transcendentals=0),
        name="input_gradient",
    )(send_rows, weight, own, *returned, *arrived)
    return (output, grad_features, grad_weight)


def solution(mesh):
    placed = (
        P(("dom", "rep"), None),
        P(),
        P(("dom", "rep"), None),
        P(("dom", "rep"), None, None, None),
        P(("dom", "rep")),
        P(("dom", "rep"), None, None),
        P(("dom", "rep"), None),
        P(("dom", "rep"), None),
    )
    return jax.shard_map(
        body,
        mesh=mesh,
        in_specs=placed,
        out_specs=(P(("dom", "rep"), None), P(("dom", "rep"), None), P()),
        check_vma=False,
    )
```

```python
import functools

import jax
import jax.numpy as jnp
from jax import lax
from jax.experimental import pallas as pl
from jax.experimental.pallas import tpu as pltpu
from jax.sharding import PartitionSpec as P

TILE = 128
F32 = jnp.float32
BF16 = jnp.bfloat16
VMEM = pl.BlockSpec(memory_space=pltpu.VMEM)
HBM = pl.BlockSpec(memory_space=pltpu.HBM)
SMEM = pl.BlockSpec(memory_space=pltpu.SMEM)


def dot(a, b, contract_a, contract_b):
    return lax.dot_general(
        a, b, (((contract_a,), (contract_b,)), ((), ())), preferred_element_type=F32
    )


def target(me, shift, count):
    return me ^ shift if count & (count - 1) == 0 else (me + shift) % count


def source(me, shift, count):
    return me ^ shift if count & (count - 1) == 0 else (me - shift + count) % count


def wanted_rows(index_ref, rows, order):
    flat = jnp.concatenate([index_ref[0, pl.ds(q, 1), :] for q in order], axis=1)
    at = lax.broadcasted_iota(jnp.int32, (rows, flat.shape[1]), 0)
    return jnp.where(at == flat, 1.0, 0.0).astype(BF16)


def pick_kernel(index_ref, features_ref, *refs):
    count = (len(refs) - 5) // 2
    loads, send_ref, keep_ref, loaded = refs[:count], refs[count], refs[count + 1], refs[count + 2 : -3]
    index, features, sems = refs[-3:]
    pairs = [(index_ref, index), (features_ref, features), *zip(loads, loaded)]
    copies = [pltpu.make_async_copy(*pair, sems.at[at]) for at, pair in enumerate(pairs)]
    for copy in copies:
        copy.start()
    here = lax.axis_index("dom")
    groups, each = index_ref.shape[1:]
    copies[0].wait()
    onehot = wanted_rows(index, features_ref.shape[0], [here ^ s for s in range(groups)])
    copies[1].wait()
    picked = dot(onehot, features[...], 0, 0).astype(BF16)
    for s in range(groups):
        to_ref = send_ref if s % 2 else keep_ref
        to_ref[s // 2 * each : (s // 2 + 1) * each, :] = picked[s * each : (s + 1) * each]
    for copy in copies[2:]:
        copy.wait()


def stage_kernel(each, keep_ref, came_ref, *outs):
    for j, out_ref in enumerate(outs):
        out_ref[:each, :] = keep_ref[j * each : (j + 1) * each, :]
        out_ref[each:, :] = came_ref[j * each : (j + 1) * each, :]


def weighted_stage_kernel(each, keep_ref, half_ref, came_ref, own_ref, share_ref, *refs):
    outs, summed = refs[:-1], refs[-1]
    pairs = len(outs) + 1
    summed[...] = half_ref[...] + came_ref[pairs * each :, :].astype(F32)
    share = summed.shape[0] // pairs
    chip = lax.axis_index("dom") // 2
    for j in range(pairs):
        to_ref = outs[j - 1] if j else own_ref
        to_ref[:each, :] = keep_ref[j * each : (j + 1) * each, :]
        to_ref[each : 2 * each, :] = came_ref[j * each : (j + 1) * each, :]
        part = summed[pl.ds(pl.multiple_of((chip ^ j) * share, share), share), :]
        if j:
            to_ref[2 * each :, :] = part.astype(BF16)
        else:
            share_ref[...] = part


def share_sum_kernel(each, share_ref, *refs):
    total = share_ref[...]
    for ref in refs[:-1]:
        total = total + ref[2 * each :, :].astype(F32)
    refs[-1][...] = total.astype(BF16)


def half_kernel(*refs):
    shares, out_ref, whole = refs[:-2], refs[-2], refs[-1]
    share = shares[0].shape[0]
    chip = lax.axis_index("dom") // 2
    for j, ref in enumerate(shares):
        whole[pl.ds(pl.multiple_of((chip ^ j) * share, share), share), :] = ref[...].astype(F32)
    out_ref[...] = whole[...].astype(BF16)


def live_tiles(counts_ref, vals_ref, t):
    return [
        jnp.where(k < counts_ref[t], vals_ref[t, k], jnp.zeros_like(vals_ref[t, k]))
        for k in range(vals_ref.shape[1])
    ]


def layer_kernel(rep, pairs, cols_ref, counts_ref, vals_ref, bnd_ref, cot_ref, weight_ref, *refs):
    blocks = refs[:rep]
    received_refs = refs[rep : rep + pairs]
    out_ref, grad_ref, send_ref, keep_ref, half_ref, panel, received, boundary, partial = refs[rep + pairs :]
    here = lax.axis_index("dom")
    me = lax.axis_index("rep")
    tiles, slots = cols_ref.shape
    for shift, block in enumerate(blocks):
        owner = source(me, shift, rep)
        for t in range(tiles):
            panel[owner * tiles + t] = block[t * TILE : (t + 1) * TILE, :]
    each = received_refs[0].shape[0] // 2
    groups = 2 * pairs

    def rows_of(group):
        return pl.ds(pl.multiple_of(group * each, each), each)

    for o in range(groups):
        received[rows_of(here ^ o), :] = received_refs[o // 2][o % 2 * each : (o % 2 + 1) * each, :]
    forward = []
    backward = []
    for t in range(tiles):
        live = live_tiles(counts_ref, vals_ref, t)
        chosen = jnp.concatenate([panel[cols_ref[t, k]] for k in range(slots)], axis=0)
        forward.append(dot(jnp.concatenate(live, axis=1), chosen, 1, 0))
        backward.append(dot(jnp.concatenate(live, axis=0), chosen, 0, 0))
    outside = dot(bnd_ref[...], received[...], 1, 0)
    mixed = jnp.concatenate(forward, axis=0) + outside
    turned = (jnp.concatenate(backward, axis=0) + outside).astype(BF16)
    high = mixed.astype(BF16)
    low = (mixed - high.astype(F32)).astype(BF16)
    weight = weight_ref[...]
    pre = dot(high, weight, 1, 0) + dot(low, weight, 1, 0)
    sig = jax.nn.sigmoid(pre)
    out_ref[...] = (pre * sig).astype(BF16)
    grad = (cot_ref[...].astype(F32) * sig * (1.0 + pre * (1.0 - sig))).astype(BF16)
    grad_ref[...] = grad
    boundary[...] = dot(bnd_ref[...], grad, 0, 0).astype(BF16)
    for s in range(groups):
        to_ref = send_ref if s % 2 else keep_ref
        to_ref[s // 2 * each : (s // 2 + 1) * each, :] = boundary[rows_of(here ^ s), :]
    partial[...] = dot(turned, grad, 0, 0)
    half = half_ref.shape[0]
    mine = here % 2
    half_ref[...] = partial[pl.ds(pl.multiple_of(mine * half, half), half), :]
    send_ref[pairs * each :, :] = partial[pl.ds(pl.multiple_of((1 - mine) * half, half), half), :].astype(BF16)


def terms_kernel(rep, layout, cols_ref, counts_ref, vals_ref, grad_ref, order_ref, *refs):
    del order_ref
    outs, terms = refs[:-1], refs[-1]
    me = lax.axis_index("rep")
    tiles, slots = cols_ref.shape
    terms[...] = jnp.zeros_like(terms)
    for t in range(tiles):
        stacked = jnp.concatenate(live_tiles(counts_ref, vals_ref, t), axis=0)
        parts = dot(stacked, grad_ref[t * TILE : (t + 1) * TILE, :], 1, 0)
        for k in range(slots):
            terms[cols_ref[t, k]] += parts[k * TILE : (k + 1) * TILE]
    for out_ref, shifts in zip(outs, layout):
        for at, shift in enumerate(shifts):
            owner = target(me, shift, rep)
            for t in range(tiles):
                row = (at * tiles + t) * TILE
                out_ref[row : row + TILE, :] = terms[owner * tiles + t].astype(out_ref.dtype)


def relay_kernel(far_ref, came_ref, *refs):
    out_ref = refs[-1]
    rows = far_ref.shape[0]
    out_ref[...] = (far_ref[...] + came_ref[rows:, :].astype(F32)).astype(BF16)


def rep_sum_kernel(*refs):
    chunk, one, two, three = [ref[...].astype(F32) for ref in refs[:4]]
    refs[-1][...] = ((chunk + two) + (one + three)).astype(BF16)


def join_kernel(bit, own_ref, got_ref, order_ref, out_ref):
    del order_ref
    own, got = own_ref[...], got_ref[...]
    half = own.shape[0]
    upper = lax.rem(lax.axis_index("dom") // bit, 2) == 1
    out_ref[:half, :] = jnp.where(upper, got, own).astype(out_ref.dtype)
    out_ref[half:, :] = jnp.where(upper, own, got).astype(out_ref.dtype)


def final_kernel(pairs, index_ref, weight_ref, own_ref, *refs):
    returned, arrived, out_ref = refs[:pairs], refs[pairs:-1], refs[-1]
    groups, each = index_ref.shape[1:]
    here = lax.axis_index("dom")
    onehot = wanted_rows(index_ref, own_ref.shape[0], [here ^ o for o in range(groups)])
    returned = jnp.concatenate([ref[: 2 * each, :] for ref in returned], axis=0)
    total = own_ref[...] + dot(onehot, returned, 1, 0)
    for term in arrived:
        total = total + term[: own_ref.shape[0], :].astype(F32)
    out_ref[...] = dot(total.astype(BF16), weight_ref[...], 1, 1).astype(BF16)


def body(features, weight, tile_cols, tile_vals, tile_counts, send_rows, bnd_adj, cotangent):
    rows, feats = features.shape
    width = weight.shape[1]
    tiles, slots = tile_cols.shape
    groups, each = send_rows.shape[1], send_rows.shape[2]
    rep = lax.axis_size("rep")
    share = feats // groups
    pairs = groups // 2
    params = pltpu.CompilerParams(vmem_limit_bytes=40 * 1024 * 1024)

    def shifted(value, shift):
        return lax.ppermute(value, "rep", [(i, target(i, shift, rep)) for i in range(rep)])

    def across(value, bits):
        return lax.ppermute(value, "dom", [(i, i ^ bits) for i in range(groups)])

    def call(kernel, name, outs, operands, scratch=(), flops=1):
        return pl.pallas_call(
            kernel,
            out_shape=outs,
            in_specs=[VMEM] * len(operands),
            out_specs=[VMEM] * len(outs),
            scratch_shapes=scratch,
            compiler_params=params,
            cost_estimate=pl.CostEstimate(flops=flops, bytes_accessed=1, transcendentals=0),
            name=name,
        )(*operands)

    def shape(high, kind=BF16, wide=width):
        return jax.ShapeDtypeStruct((high, wide), kind)

    blocks = [features] + [shifted(features, shift) for shift in range(1, rep)]
    loads = [tile_vals, cotangent, tile_cols, tile_counts]
    send, keep, tile_vals, cotangent, tile_cols, tile_counts = pl.pallas_call(
        pick_kernel,
        out_shape=[
            *[shape(pairs * each, BF16, feats)] * 2,
            *[jax.ShapeDtypeStruct(load.shape, load.dtype) for load in loads],
        ],
        in_specs=[HBM] * (2 + len(loads)),
        out_specs=[VMEM] * (2 + len(loads)),
        scratch_shapes=[
            pltpu.VMEM(send_rows.shape, jnp.int32),
            pltpu.VMEM((rows, feats), BF16),
            pltpu.SemaphoreType.DMA((2 + len(loads),)),
        ],
        compiler_params=params,
        name="pick_rows",
    )(*[pltpu.with_memory_space_constraint(x, pltpu.HBM) for x in (send_rows, features, *loads)])
    received = call(
        functools.partial(stage_kernel, each),
        "pair_rows",
        [shape(2 * each, BF16, feats)] * pairs,
        (keep, across(send, 1)),
    )
    received = [received[0]] + [across(received[j], 2 * j) for j in range(1, pairs)]
    half = feats // 2
    output, grad, send, keep, mine = pl.pallas_call(
        functools.partial(layer_kernel, rep, pairs),
        out_shape=[
            shape(rows),
            shape(rows),
            shape(pairs * each + half),
            shape(pairs * each),
            shape(half, F32),
        ],
        in_specs=[SMEM] * 2 + [VMEM] * (4 + rep + pairs),
        out_specs=[VMEM] * 5,
        scratch_shapes=[
            pltpu.VMEM((rep * tiles, TILE, feats), BF16),
            pltpu.VMEM((groups * each, feats), BF16),
            pltpu.VMEM((groups * each, width), BF16),
            pltpu.VMEM((feats, width), F32),
        ],
        compiler_params=params,
        name="layer",
    )(tile_cols, tile_counts, tile_vals, bnd_adj, cotangent, weight, *blocks, *received)
    own_rows, own_share, *parts = call(
        functools.partial(weighted_stage_kernel, each),
        "pair_gradients",
        [shape(2 * each), shape(share, F32)] + [shape(2 * each + share)] * (pairs - 1),
        (keep, mine, across(send, 1)),
        [pltpu.VMEM((half, width), F32)],
    )
    parts = [across(part, 2 * j) for j, part in enumerate(parts, 1)]
    returned = [own_rows] + parts
    relayed = rep == 4
    layout = [(0,), (1, 3), (2,)] if relayed else [(shift,) for shift in range(rep)]
    kinds = [F32, BF16, F32] if relayed else [F32] + [BF16] * (rep - 1)
    own, *sends = pl.pallas_call(
        functools.partial(terms_kernel, rep, layout),
        out_shape=[
            jax.ShapeDtypeStruct((len(shifts) * rows, width), kind)
            for shifts, kind in zip(layout, kinds)
        ],
        in_specs=[SMEM] * 2 + [VMEM] * 3,
        out_specs=[VMEM] * len(layout),
        scratch_shapes=[pltpu.VMEM((rep * tiles, TILE, width), F32)],
        compiler_params=params,
        cost_estimate=pl.CostEstimate(flops=500000001, bytes_accessed=1, transcendentals=0),
        name="terms",
    )(tile_cols, tile_counts, tile_vals, grad, own_rows)
    (chunk,) = call(
        functools.partial(share_sum_kernel, each), "share_sum", [shape(share)], (own_share, *parts), flops=4000000001
    )
    if relayed:
        came = shifted(sends[0], 1)
        small = [shifted(chunk, shift) for shift in (1, 2, 3)]
        (relay,) = call(relay_kernel, "relay", [shape(rows)], (sends[1], came, chunk))
        arrived = [came, shifted(relay, 2)]
        (piece,) = call(rep_sum_kernel, "rep_sum", [shape(share)], (chunk, *small), flops=1000000001)
    else:
        arrived = [shifted(send, shift) for shift, send in enumerate(sends, 1)]
        piece = jnp.sum(lax.all_gather(chunk, "rep").astype(F32), axis=0).astype(BF16)
    pieces = [piece] + [across(piece, 2 * j) for j in range(1, pairs)]
    (piece,) = call(half_kernel, "half", [shape(half)], pieces, [pltpu.VMEM((half, width), F32)], 1)
    grad_features = pl.pallas_call(
        functools.partial(final_kernel, pairs),
        out_shape=jax.ShapeDtypeStruct((rows, feats), BF16),
        in_specs=[VMEM] * (3 + pairs + len(arrived)),
        out_specs=VMEM,
        compiler_params=params,
        cost_estimate=pl.CostEstimate(flops=1, bytes_accessed=1, transcendentals=0),
        name="input_gradient",
    )(send_rows, weight, own, *returned, *arrived)
    grad_weight = pl.pallas_call(
        functools.partial(join_kernel, 1),
        out_shape=shape(feats, F32),
        in_specs=[VMEM, VMEM, HBM],
        out_specs=VMEM,
        compiler_params=params,
        cost_estimate=pl.CostEstimate(flops=1, bytes_accessed=1, transcendentals=0),
        name="join",
    )(piece, across(piece, 1), pltpu.with_memory_space_constraint(grad_features, pltpu.HBM))
    return (output, grad_features, grad_weight)


def solution(mesh):
    placed = (
        P(("dom", "rep"), None),
        P(),
        P(("dom", "rep"), None),
        P(("dom", "rep"), None, None, None),
        P(("dom", "rep")),
        P(("dom", "rep"), None, None),
        P(("dom", "rep"), None),
        P(("dom", "rep"), None),
    )
    return jax.shard_map(
        body,
        mesh=mesh,
        in_specs=placed,
        out_specs=(P(("dom", "rep"), None), P(("dom", "rep"), None), P()),
        check_vma=False,
    )
```

```python
import functools

import jax
import jax.numpy as jnp
from jax import lax
from jax.experimental import pallas as pl
from jax.experimental.pallas import tpu as pltpu
from jax.sharding import PartitionSpec as P

TILE = 128
F32 = jnp.float32
BF16 = jnp.bfloat16
VMEM = pl.BlockSpec(memory_space=pltpu.VMEM)
HBM = pl.BlockSpec(memory_space=pltpu.HBM)
SMEM = pl.BlockSpec(memory_space=pltpu.SMEM)


def dot(a, b, contract_a, contract_b):
    return lax.dot_general(
        a, b, (((contract_a,), (contract_b,)), ((), ())), preferred_element_type=F32
    )


def target(me, shift, count):
    return me ^ shift if count & (count - 1) == 0 else (me + shift) % count


def source(me, shift, count):
    return me ^ shift if count & (count - 1) == 0 else (me - shift + count) % count


def wanted_rows(index_ref, rows, order):
    flat = jnp.concatenate([index_ref[0, pl.ds(q, 1), :] for q in order], axis=1)
    at = lax.broadcasted_iota(jnp.int32, (rows, flat.shape[1]), 0)
    return jnp.where(at == flat, 1.0, 0.0).astype(BF16)


def pick_kernel(index_ref, features_ref, *refs):
    count = (len(refs) - 5) // 2
    loads, send_ref, keep_ref, index, loaded = refs[:count], *refs[count : count + 3], refs[count + 3 : -2]
    features, sems = refs[-2:]
    pairs = [(index_ref, index), (features_ref, features), *zip(loads, loaded)]
    copies = [pltpu.make_async_copy(*pair, sems.at[at]) for at, pair in enumerate(pairs)]
    for copy in copies:
        copy.start()
    here = lax.axis_index("dom")
    groups, each = index_ref.shape[1:]
    copies[0].wait()
    onehot = wanted_rows(index, features_ref.shape[0], [here ^ s for s in range(groups)])
    copies[1].wait()
    picked = dot(onehot, features[...], 0, 0).astype(BF16)
    for s in range(groups):
        to_ref = send_ref if s % 2 else keep_ref
        to_ref[s // 2 * each : (s // 2 + 1) * each, :] = picked[s * each : (s + 1) * each]
    for copy in copies[2:]:
        copy.wait()


def stage_kernel(each, keep_ref, came_ref, *outs):
    for j, out_ref in enumerate(outs):
        out_ref[:each, :] = keep_ref[j * each : (j + 1) * each, :]
        out_ref[each:, :] = came_ref[j * each : (j + 1) * each, :]


def weighted_stage_kernel(each, keep_ref, half_ref, came_ref, own_ref, share_ref, *refs):
    outs, summed = refs[:-1], refs[-1]
    pairs = len(outs) + 1
    summed[...] = half_ref[...] + came_ref[pairs * each :, :].astype(F32)
    share = summed.shape[0] // pairs
    chip = lax.axis_index("dom") // 2
    for j in range(pairs):
        to_ref = outs[j - 1] if j else own_ref
        to_ref[:each, :] = keep_ref[j * each : (j + 1) * each, :]
        to_ref[each : 2 * each, :] = came_ref[j * each : (j + 1) * each, :]
        part = summed[pl.ds(pl.multiple_of((chip ^ j) * share, share), share), :]
        if j:
            to_ref[2 * each :, :] = part.astype(BF16)
        else:
            share_ref[...] = part


def share_sum_kernel(each, share_ref, *refs):
    total = share_ref[...]
    for ref in refs[:-1]:
        total = total + ref[2 * each :, :].astype(F32)
    refs[-1][...] = total.astype(BF16)


def half_kernel(*refs):
    shares, out_ref, whole = refs[:-2], refs[-2], refs[-1]
    share = shares[0].shape[0]
    chip = lax.axis_index("dom") // 2
    for j, ref in enumerate(shares):
        whole[pl.ds(pl.multiple_of((chip ^ j) * share, share), share), :] = ref[...].astype(F32)
    out_ref[...] = whole[...].astype(BF16)


def live_tiles(counts_ref, vals_ref, t):
    return [
        jnp.where(k < counts_ref[t], vals_ref[t, k], jnp.zeros_like(vals_ref[t, k]))
        for k in range(vals_ref.shape[1])
    ]


def layer_kernel(rep, pairs, cols_ref, counts_ref, vals_ref, bnd_ref, cot_ref, weight_ref, *refs):
    blocks = refs[:rep]
    received_refs = refs[rep : rep + pairs]
    out_ref, grad_ref, send_ref, keep_ref, half_ref, panel, received, boundary, partial = refs[rep + pairs :]
    here = lax.axis_index("dom")
    me = lax.axis_index("rep")
    tiles, slots = cols_ref.shape
    for shift, block in enumerate(blocks):
        owner = source(me, shift, rep)
        for t in range(tiles):
            panel[owner * tiles + t] = block[t * TILE : (t + 1) * TILE, :]
    each = received_refs[0].shape[0] // 2
    groups = 2 * pairs

    def rows_of(group):
        return pl.ds(pl.multiple_of(group * each, each), each)

    for o in range(groups):
        received[rows_of(here ^ o), :] = received_refs[o // 2][o % 2 * each : (o % 2 + 1) * each, :]
    forward = []
    backward = []
    for t in range(tiles):
        live = live_tiles(counts_ref, vals_ref, t)
        chosen = jnp.concatenate([panel[cols_ref[t, k]] for k in range(slots)], axis=0)
        forward.append(dot(jnp.concatenate(live, axis=1), chosen, 1, 0))
        backward.append(dot(jnp.concatenate(live, axis=0), chosen, 0, 0))
    outside = dot(bnd_ref[...], received[...], 1, 0)
    mixed = jnp.concatenate(forward, axis=0) + outside
    turned = (jnp.concatenate(backward, axis=0) + outside).astype(BF16)
    high = mixed.astype(BF16)
    low = (mixed - high.astype(F32)).astype(BF16)
    weight = weight_ref[...]
    pre = dot(high, weight, 1, 0) + dot(low, weight, 1, 0)
    sig = jax.nn.sigmoid(pre)
    out_ref[...] = (pre * sig).astype(BF16)
    grad = (cot_ref[...].astype(F32) * sig * (1.0 + pre * (1.0 - sig))).astype(BF16)
    grad_ref[...] = grad
    boundary[...] = dot(bnd_ref[...], grad, 0, 0).astype(BF16)
    for s in range(groups):
        to_ref = send_ref if s % 2 else keep_ref
        to_ref[s // 2 * each : (s // 2 + 1) * each, :] = boundary[rows_of(here ^ s), :]
    partial[...] = dot(turned, grad, 0, 0)
    half = half_ref.shape[0]
    mine = here % 2
    half_ref[...] = partial[pl.ds(pl.multiple_of(mine * half, half), half), :]
    send_ref[pairs * each :, :] = partial[pl.ds(pl.multiple_of((1 - mine) * half, half), half), :].astype(BF16)


def terms_kernel(rep, layout, cols_ref, counts_ref, vals_ref, grad_ref, order_ref, *refs):
    del order_ref
    outs, terms = refs[:-1], refs[-1]
    me = lax.axis_index("rep")
    tiles, slots = cols_ref.shape
    terms[...] = jnp.zeros_like(terms)
    for t in range(tiles):
        stacked = jnp.concatenate(live_tiles(counts_ref, vals_ref, t), axis=0)
        parts = dot(stacked, grad_ref[t * TILE : (t + 1) * TILE, :], 1, 0)
        for k in range(slots):
            terms[cols_ref[t, k]] += parts[k * TILE : (k + 1) * TILE]
    for out_ref, shifts in zip(outs, layout):
        for at, shift in enumerate(shifts):
            owner = target(me, shift, rep)
            for t in range(tiles):
                row = (at * tiles + t) * TILE
                out_ref[row : row + TILE, :] = terms[owner * tiles + t].astype(out_ref.dtype)


def relay_kernel(far_ref, came_ref, *refs):
    out_ref = refs[-1]
    rows = far_ref.shape[0]
    out_ref[...] = (far_ref[...] + came_ref[rows:, :].astype(F32)).astype(BF16)


def pair_sum_kernel(own_ref, came_ref, out_ref):
    out_ref[...] = (own_ref[...].astype(F32) + came_ref[...].astype(F32)).astype(BF16)


def join_kernel(bit, own_ref, got_ref, order_ref, out_ref):
    del order_ref
    own, got = own_ref[...], got_ref[...]
    half = own.shape[0]
    upper = lax.rem(lax.axis_index("dom") // bit, 2) == 1
    out_ref[:half, :] = jnp.where(upper, got, own).astype(out_ref.dtype)
    out_ref[half:, :] = jnp.where(upper, own, got).astype(out_ref.dtype)


def final_kernel(pairs, index_ref, weight_ref, own_ref, *refs):
    returned, arrived, out_ref = refs[:pairs], refs[pairs:-1], refs[-1]
    groups, each = index_ref.shape[1:]
    here = lax.axis_index("dom")
    onehot = wanted_rows(index_ref, own_ref.shape[0], [here ^ o for o in range(groups)])
    returned = jnp.concatenate([ref[: 2 * each, :] for ref in returned], axis=0)
    total = own_ref[...] + dot(onehot, returned, 1, 0)
    for term in arrived:
        total = total + term[: own_ref.shape[0], :].astype(F32)
    out_ref[...] = dot(total.astype(BF16), weight_ref[...], 1, 1).astype(BF16)


def body(features, weight, tile_cols, tile_vals, tile_counts, send_rows, bnd_adj, cotangent):
    rows, feats = features.shape
    width = weight.shape[1]
    tiles, slots = tile_cols.shape
    groups, each = send_rows.shape[1], send_rows.shape[2]
    rep = lax.axis_size("rep")
    share = feats // groups
    pairs = groups // 2
    params = pltpu.CompilerParams(vmem_limit_bytes=40 * 1024 * 1024)

    def shifted(value, shift):
        return lax.ppermute(value, "rep", [(i, target(i, shift, rep)) for i in range(rep)])

    def across(value, bits):
        return lax.ppermute(value, "dom", [(i, i ^ bits) for i in range(groups)])

    def call(kernel, name, outs, operands, scratch=(), flops=1):
        return pl.pallas_call(
            kernel,
            out_shape=outs,
            in_specs=[VMEM] * len(operands),
            out_specs=[VMEM] * len(outs),
            scratch_shapes=scratch,
            compiler_params=params,
            cost_estimate=pl.CostEstimate(flops=flops, bytes_accessed=1, transcendentals=0),
            name=name,
        )(*operands)

    def shape(high, kind=BF16, wide=width):
        return jax.ShapeDtypeStruct((high, wide), kind)

    blocks = [features] + [shifted(features, shift) for shift in range(1, rep)]
    relayed = rep == 4
    loads = [tile_vals, cotangent, tile_cols, tile_counts]
    send, keep, index, tile_vals, cotangent, tile_cols, tile_counts = pl.pallas_call(
        pick_kernel,
        out_shape=[
            *[shape(pairs * each, BF16, feats)] * 2,
            jax.ShapeDtypeStruct(send_rows.shape, jnp.int32),
            *[jax.ShapeDtypeStruct(load.shape, load.dtype) for load in loads],
        ],
        in_specs=[HBM] * (2 + len(loads)),
        out_specs=[VMEM] * (3 + len(loads)),
        scratch_shapes=[
            pltpu.VMEM((rows, feats), BF16),
            pltpu.SemaphoreType.DMA((2 + len(loads),)),
        ],
        compiler_params=params,
        name="pick_rows",
    )(*[pltpu.with_memory_space_constraint(x, pltpu.HBM) for x in (send_rows, features, *loads)])
    received = call(
        functools.partial(stage_kernel, each),
        "pair_rows",
        [shape(2 * each, BF16, feats)] * pairs,
        (keep, across(send, 1)),
    )
    received = [received[0]] + [across(received[j], 2 * j) for j in range(1, pairs)]
    half = feats // 2
    output, grad, send, keep, mine = pl.pallas_call(
        functools.partial(layer_kernel, rep, pairs),
        out_shape=[
            shape(rows),
            shape(rows),
            shape(pairs * each + half),
            shape(pairs * each),
            shape(half, F32),
        ],
        in_specs=[SMEM] * 2 + [VMEM] * (4 + rep + pairs),
        out_specs=[VMEM] * 5,
        scratch_shapes=[
            pltpu.VMEM((rep * tiles, TILE, feats), BF16),
            pltpu.VMEM((groups * each, feats), BF16),
            pltpu.VMEM((groups * each, width), BF16),
            pltpu.VMEM((feats, width), F32),
        ],
        compiler_params=params,
        name="layer",
    )(tile_cols, tile_counts, tile_vals, bnd_adj, cotangent, weight, *blocks, *received)
    own_rows, own_share, *parts = call(
        functools.partial(weighted_stage_kernel, each),
        "pair_gradients",
        [shape(2 * each), shape(share, F32)] + [shape(2 * each + share)] * (pairs - 1),
        (keep, mine, across(send, 1)),
        [pltpu.VMEM((half, width), F32)],
    )
    parts = [across(part, 2 * j) for j, part in enumerate(parts, 1)]
    returned = [own_rows] + parts
    layout = [(0,), (1, 3), (2,)] if relayed else [(shift,) for shift in range(rep)]
    kinds = [F32, BF16, F32] if relayed else [F32] + [BF16] * (rep - 1)
    own, *sends = pl.pallas_call(
        functools.partial(terms_kernel, rep, layout),
        out_shape=[
            jax.ShapeDtypeStruct((len(shifts) * rows, width), kind)
            for shifts, kind in zip(layout, kinds)
        ],
        in_specs=[SMEM] * 2 + [VMEM] * 3,
        out_specs=[VMEM] * len(layout),
        scratch_shapes=[pltpu.VMEM((rep * tiles, TILE, width), F32)],
        compiler_params=params,
        cost_estimate=pl.CostEstimate(flops=500000001, bytes_accessed=1, transcendentals=0),
        name="terms",
    )(tile_cols, tile_counts, tile_vals, grad, own_rows)
    (chunk,) = call(
        functools.partial(share_sum_kernel, each), "share_sum", [shape(share)], (own_share, *parts), flops=4000000001
    )
    if relayed:
        came = shifted(sends[0], 1)
        (near,) = call(
            pair_sum_kernel, "pair_sum", [shape(share)], (chunk, shifted(chunk, 1)), flops=1000000001
        )
        (piece,) = call(
            pair_sum_kernel, "rep_sum", [shape(share)], (near, shifted(near, 2)), flops=1000000001
        )
        (relay,) = call(relay_kernel, "relay", [shape(rows)], (sends[1], came, near))
        arrived = [came, shifted(relay, 2)]
    else:
        arrived = [shifted(send, shift) for shift, send in enumerate(sends, 1)]
        piece = jnp.sum(lax.all_gather(chunk, "rep").astype(F32), axis=0).astype(BF16)
    pieces = [piece] + [across(piece, 2 * j) for j in range(1, pairs)]
    (piece,) = call(half_kernel, "half", [shape(half)], pieces, [pltpu.VMEM((half, width), F32)], 1)
    grad_features = pl.pallas_call(
        functools.partial(final_kernel, pairs),
        out_shape=jax.ShapeDtypeStruct((rows, feats), BF16),
        in_specs=[VMEM] * (3 + pairs + len(arrived)),
        out_specs=VMEM,
        compiler_params=params,
        cost_estimate=pl.CostEstimate(flops=1, bytes_accessed=1, transcendentals=0),
        name="input_gradient",
    )(index, weight, own, *returned, *arrived)
    grad_weight = pl.pallas_call(
        functools.partial(join_kernel, 1),
        out_shape=shape(feats, F32),
        in_specs=[VMEM, VMEM, HBM],
        out_specs=VMEM,
        compiler_params=params,
        cost_estimate=pl.CostEstimate(flops=1, bytes_accessed=1, transcendentals=0),
        name="join",
    )(piece, across(piece, 1), pltpu.with_memory_space_constraint(grad_features, pltpu.HBM))
    return (output, grad_features, grad_weight)


def solution(mesh):
    placed = (
        P(("dom", "rep"), None),
        P(),
        P(("dom", "rep"), None),
        P(("dom", "rep"), None, None, None),
        P(("dom", "rep")),
        P(("dom", "rep"), None, None),
        P(("dom", "rep"), None),
        P(("dom", "rep"), None),
    )
    return jax.shard_map(
        body,
        mesh=mesh,
        in_specs=placed,
        out_specs=(P(("dom", "rep"), None), P(("dom", "rep"), None), P()),
        check_vma=False,
    )
```

```python
import functools

import jax
import jax.numpy as jnp
from jax import lax
from jax.experimental import pallas as pl
from jax.experimental.pallas import tpu as pltpu
from jax.sharding import PartitionSpec as P

TILE = 128
F32 = jnp.float32
BF16 = jnp.bfloat16
VMEM = pl.BlockSpec(memory_space=pltpu.VMEM)
HBM = pl.BlockSpec(memory_space=pltpu.HBM)
SMEM = pl.BlockSpec(memory_space=pltpu.SMEM)


def dot(a, b, contract_a, contract_b):
    return lax.dot_general(
        a, b, (((contract_a,), (contract_b,)), ((), ())), preferred_element_type=F32
    )


def target(me, shift, count):
    return me ^ shift if count & (count - 1) == 0 else (me + shift) % count


def source(me, shift, count):
    return me ^ shift if count & (count - 1) == 0 else (me - shift + count) % count


def wanted_rows(index_ref, rows, order):
    flat = jnp.concatenate([index_ref[0, pl.ds(q, 1), :] for q in order], axis=1)
    at = lax.broadcasted_iota(jnp.int32, (rows, flat.shape[1]), 0)
    return jnp.where(at == flat, 1.0, 0.0).astype(BF16)


def pick_kernel(index_ref, features_ref, *refs):
    count = (len(refs) - 5) // 2
    loads, send_ref, keep_ref, index, loaded = refs[:count], *refs[count : count + 3], refs[count + 3 : -2]
    features, sems = refs[-2:]
    pairs = [(index_ref, index), (features_ref, features), *zip(loads, loaded)]
    copies = [pltpu.make_async_copy(*pair, sems.at[at]) for at, pair in enumerate(pairs)]
    for copy in copies:
        copy.start()
    here = lax.axis_index("dom")
    groups, each = index_ref.shape[1:]
    copies[0].wait()
    onehot = wanted_rows(index, features_ref.shape[0], [here ^ s for s in range(groups)])
    copies[1].wait()
    picked = dot(onehot, features[...], 0, 0).astype(BF16)
    for s in range(groups):
        to_ref = send_ref if s % 2 else keep_ref
        to_ref[s // 2 * each : (s // 2 + 1) * each, :] = picked[s * each : (s + 1) * each]
    for copy in copies[2:]:
        copy.wait()


def stage_kernel(each, keep_ref, came_ref, *outs):
    for j, out_ref in enumerate(outs):
        out_ref[:each, :] = keep_ref[j * each : (j + 1) * each, :]
        out_ref[each:, :] = came_ref[j * each : (j + 1) * each, :]


def weighted_stage_kernel(each, keep_ref, half_ref, came_ref, order_ref, own_ref, share_ref, *refs):
    del order_ref
    outs, summed = refs[:-1], refs[-1]
    pairs = len(outs) + 1
    summed[...] = half_ref[...] + came_ref[pairs * each :, :].astype(F32)
    share = summed.shape[0] // pairs
    chip = lax.axis_index("dom") // 2
    for j in range(pairs):
        to_ref = outs[j - 1] if j else own_ref
        to_ref[:each, :] = keep_ref[j * each : (j + 1) * each, :]
        to_ref[each : 2 * each, :] = came_ref[j * each : (j + 1) * each, :]
        part = summed[pl.ds(pl.multiple_of((chip ^ j) * share, share), share), :]
        if j:
            to_ref[2 * each :, :] = part.astype(BF16)
        else:
            share_ref[...] = part


def share_sum_kernel(each, share_ref, *refs):
    total = share_ref[...]
    for ref in refs[:-1]:
        total = total + ref[2 * each :, :].astype(F32)
    refs[-1][...] = total.astype(BF16)


def half_kernel(*refs):
    shares, out_ref, whole = refs[:-2], refs[-2], refs[-1]
    share = shares[0].shape[0]
    chip = lax.axis_index("dom") // 2
    for j, ref in enumerate(shares):
        whole[pl.ds(pl.multiple_of((chip ^ j) * share, share), share), :] = ref[...].astype(F32)
    out_ref[...] = whole[...].astype(BF16)


def live_tiles(counts_ref, vals_ref, t):
    return [
        jnp.where(k < counts_ref[t], vals_ref[t, k], jnp.zeros_like(vals_ref[t, k]))
        for k in range(vals_ref.shape[1])
    ]


def layer_kernel(rep, pairs, cols_ref, counts_ref, vals_ref, bnd_ref, cot_ref, weight_ref, *refs):
    blocks = refs[:rep]
    received_refs = refs[rep : rep + pairs]
    out_ref, grad_ref, send_ref, keep_ref, half_ref, panel, received, boundary, partial = refs[rep + pairs :]
    here = lax.axis_index("dom")
    me = lax.axis_index("rep")
    tiles, slots = cols_ref.shape
    for shift, block in enumerate(blocks):
        owner = source(me, shift, rep)
        for t in range(tiles):
            panel[owner * tiles + t] = block[t * TILE : (t + 1) * TILE, :]
    each = received_refs[0].shape[0] // 2
    groups = 2 * pairs

    def rows_of(group):
        return pl.ds(pl.multiple_of(group * each, each), each)

    for o in range(groups):
        received[rows_of(here ^ o), :] = received_refs[o // 2][o % 2 * each : (o % 2 + 1) * each, :]
    forward = []
    backward = []
    for t in range(tiles):
        live = live_tiles(counts_ref, vals_ref, t)
        chosen = jnp.concatenate([panel[cols_ref[t, k]] for k in range(slots)], axis=0)
        forward.append(dot(jnp.concatenate(live, axis=1), chosen, 1, 0))
        backward.append(dot(jnp.concatenate(live, axis=0), chosen, 0, 0))
    outside = dot(bnd_ref[...], received[...], 1, 0)
    mixed = jnp.concatenate(forward, axis=0) + outside
    turned = (jnp.concatenate(backward, axis=0) + outside).astype(BF16)
    high = mixed.astype(BF16)
    low = (mixed - high.astype(F32)).astype(BF16)
    weight = weight_ref[...]
    pre = dot(high, weight, 1, 0) + dot(low, weight, 1, 0)
    sig = jax.nn.sigmoid(pre)
    out_ref[...] = (pre * sig).astype(BF16)
    grad = (cot_ref[...].astype(F32) * sig * (1.0 + pre * (1.0 - sig))).astype(BF16)
    grad_ref[...] = grad
    boundary[...] = dot(bnd_ref[...], grad, 0, 0).astype(BF16)
    for s in range(groups):
        to_ref = send_ref if s % 2 else keep_ref
        to_ref[s // 2 * each : (s // 2 + 1) * each, :] = boundary[rows_of(here ^ s), :]
    partial[...] = dot(turned, grad, 0, 0)
    half = half_ref.shape[0]
    mine = here % 2
    half_ref[...] = partial[pl.ds(pl.multiple_of(mine * half, half), half), :]
    send_ref[pairs * each :, :] = partial[pl.ds(pl.multiple_of((1 - mine) * half, half), half), :].astype(BF16)


def terms_kernel(rep, layout, cols_ref, counts_ref, vals_ref, grad_ref, *refs):
    outs, terms = refs[:-1], refs[-1]
    me = lax.axis_index("rep")
    tiles, slots = cols_ref.shape
    terms[...] = jnp.zeros_like(terms)
    for t in range(tiles):
        stacked = jnp.concatenate(live_tiles(counts_ref, vals_ref, t), axis=0)
        parts = dot(stacked, grad_ref[t * TILE : (t + 1) * TILE, :], 1, 0)
        for k in range(slots):
            terms[cols_ref[t, k]] += parts[k * TILE : (k + 1) * TILE]
    for out_ref, shifts in zip(outs, layout):
        for at, shift in enumerate(shifts):
            owner = target(me, shift, rep)
            for t in range(tiles):
                row = (at * tiles + t) * TILE
                out_ref[row : row + TILE, :] = terms[owner * tiles + t].astype(out_ref.dtype)


def relay_kernel(far_ref, came_ref, *refs):
    out_ref = refs[-1]
    rows = far_ref.shape[0]
    out_ref[...] = (far_ref[...] + came_ref[rows:, :].astype(F32)).astype(BF16)


def pair_sum_kernel(own_ref, came_ref, out_ref):
    out_ref[...] = (own_ref[...].astype(F32) + came_ref[...].astype(F32)).astype(BF16)


def join_kernel(bit, own_ref, got_ref, order_ref, out_ref):
    del order_ref
    own, got = own_ref[...], got_ref[...]
    half = own.shape[0]
    upper = lax.rem(lax.axis_index("dom") // bit, 2) == 1
    out_ref[:half, :] = jnp.where(upper, got, own).astype(out_ref.dtype)
    out_ref[half:, :] = jnp.where(upper, own, got).astype(out_ref.dtype)


def final_kernel(pairs, index_ref, weight_ref, own_ref, *refs):
    returned, arrived, out_ref = refs[:pairs], refs[pairs:-1], refs[-1]
    groups, each = index_ref.shape[1:]
    here = lax.axis_index("dom")
    onehot = wanted_rows(index_ref, own_ref.shape[0], [here ^ o for o in range(groups)])
    returned = jnp.concatenate([ref[: 2 * each, :] for ref in returned], axis=0)
    total = own_ref[...] + dot(onehot, returned, 1, 0)
    for term in arrived:
        total = total + term[: own_ref.shape[0], :].astype(F32)
    out_ref[...] = dot(total.astype(BF16), weight_ref[...], 1, 1).astype(BF16)


def body(features, weight, tile_cols, tile_vals, tile_counts, send_rows, bnd_adj, cotangent):
    rows, feats = features.shape
    width = weight.shape[1]
    tiles, slots = tile_cols.shape
    groups, each = send_rows.shape[1], send_rows.shape[2]
    rep = lax.axis_size("rep")
    share = feats // groups
    pairs = groups // 2
    params = pltpu.CompilerParams(vmem_limit_bytes=40 * 1024 * 1024)

    def shifted(value, shift):
        return lax.ppermute(value, "rep", [(i, target(i, shift, rep)) for i in range(rep)])

    def across(value, bits):
        return lax.ppermute(value, "dom", [(i, i ^ bits) for i in range(groups)])

    def call(kernel, name, outs, operands, scratch=(), flops=1):
        return pl.pallas_call(
            kernel,
            out_shape=outs,
            in_specs=[VMEM] * len(operands),
            out_specs=[VMEM] * len(outs),
            scratch_shapes=scratch,
            compiler_params=params,
            cost_estimate=pl.CostEstimate(flops=flops, bytes_accessed=1, transcendentals=0),
            name=name,
        )(*operands)

    def shape(high, kind=BF16, wide=width):
        return jax.ShapeDtypeStruct((high, wide), kind)

    blocks = [features] + [shifted(features, shift) for shift in range(1, rep)]
    relayed = rep == 4
    loads = [tile_vals, cotangent, tile_cols, tile_counts]
    send, keep, index, tile_vals, cotangent, tile_cols, tile_counts = pl.pallas_call(
        pick_kernel,
        out_shape=[
            *[shape(pairs * each, BF16, feats)] * 2,
            jax.ShapeDtypeStruct(send_rows.shape, jnp.int32),
            *[jax.ShapeDtypeStruct(load.shape, load.dtype) for load in loads],
        ],
        in_specs=[HBM] * (2 + len(loads)),
        out_specs=[VMEM] * (3 + len(loads)),
        scratch_shapes=[
            pltpu.VMEM((rows, feats), BF16),
            pltpu.SemaphoreType.DMA((2 + len(loads),)),
        ],
        compiler_params=params,
        name="pick_rows",
    )(*[pltpu.with_memory_space_constraint(x, pltpu.HBM) for x in (send_rows, features, *loads)])
    received = call(
        functools.partial(stage_kernel, each),
        "pair_rows",
        [shape(2 * each, BF16, feats)] * pairs,
        (keep, across(send, 1)),
    )
    received = [received[0]] + [across(received[j], 2 * j) for j in range(1, pairs)]
    half = feats // 2
    output, grad, send, keep, mine = pl.pallas_call(
        functools.partial(layer_kernel, rep, pairs),
        out_shape=[
            shape(rows),
            shape(rows),
            shape(pairs * each + half),
            shape(pairs * each),
            shape(half, F32),
        ],
        in_specs=[SMEM] * 2 + [VMEM] * (4 + rep + pairs),
        out_specs=[VMEM] * 5,
        scratch_shapes=[
            pltpu.VMEM((rep * tiles, TILE, feats), BF16),
            pltpu.VMEM((groups * each, feats), BF16),
            pltpu.VMEM((groups * each, width), BF16),
            pltpu.VMEM((feats, width), F32),
        ],
        compiler_params=params,
        name="layer",
    )(tile_cols, tile_counts, tile_vals, bnd_adj, cotangent, weight, *blocks, *received)
    layout = [(0,), (1, 3), (2,)] if relayed else [(shift,) for shift in range(rep)]
    kinds = [F32, BF16, F32] if relayed else [F32] + [BF16] * (rep - 1)
    own, *sends = pl.pallas_call(
        functools.partial(terms_kernel, rep, layout),
        out_shape=[
            jax.ShapeDtypeStruct((len(shifts) * rows, width), kind)
            for shifts, kind in zip(layout, kinds)
        ],
        in_specs=[SMEM] * 2 + [VMEM] * 2,
        out_specs=[VMEM] * len(layout),
        scratch_shapes=[pltpu.VMEM((rep * tiles, TILE, width), F32)],
        compiler_params=params,
        cost_estimate=pl.CostEstimate(flops=500000001, bytes_accessed=1, transcendentals=0),
        name="terms",
    )(tile_cols, tile_counts, tile_vals, grad)
    own_rows, own_share, *parts = call(
        functools.partial(weighted_stage_kernel, each),
        "pair_gradients",
        [shape(2 * each), shape(share, F32)] + [shape(2 * each + share)] * (pairs - 1),
        (keep, mine, across(send, 1), own),
        [pltpu.VMEM((half, width), F32)],
    )
    parts = [across(part, 2 * j) for j, part in enumerate(parts, 1)]
    returned = [own_rows] + parts
    (chunk,) = call(
        functools.partial(share_sum_kernel, each), "share_sum", [shape(share)], (own_share, *parts), flops=1000000001
    )
    if relayed:
        came = shifted(sends[0], 1)
        (near,) = call(
            pair_sum_kernel, "pair_sum", [shape(share)], (chunk, shifted(chunk, 1)), flops=1000000001
        )
        (piece,) = call(
            pair_sum_kernel, "rep_sum", [shape(share)], (near, shifted(near, 2)), flops=1000000001
        )
        (relay,) = call(relay_kernel, "relay", [shape(rows)], (sends[1], came, near))
        arrived = [came, shifted(relay, 2)]
    else:
        arrived = [shifted(send, shift) for shift, send in enumerate(sends, 1)]
        piece = jnp.sum(lax.all_gather(chunk, "rep").astype(F32), axis=0).astype(BF16)
    pieces = [piece] + [across(piece, 2 * j) for j in range(1, pairs)]
    (piece,) = call(half_kernel, "half", [shape(half)], pieces, [pltpu.VMEM((half, width), F32)], 1)
    grad_features = pl.pallas_call(
        functools.partial(final_kernel, pairs),
        out_shape=jax.ShapeDtypeStruct((rows, feats), BF16),
        in_specs=[VMEM] * (3 + pairs + len(arrived)),
        out_specs=VMEM,
        compiler_params=params,
        cost_estimate=pl.CostEstimate(flops=1, bytes_accessed=1, transcendentals=0),
        name="input_gradient",
    )(index, weight, own, *returned, *arrived)
    grad_weight = pl.pallas_call(
        functools.partial(join_kernel, 1),
        out_shape=shape(feats, F32),
        in_specs=[VMEM, VMEM, HBM],
        out_specs=VMEM,
        compiler_params=params,
        cost_estimate=pl.CostEstimate(flops=1, bytes_accessed=1, transcendentals=0),
        name="join",
    )(piece, across(piece, 1), pltpu.with_memory_space_constraint(grad_features, pltpu.HBM))
    return (output, grad_features, grad_weight)


def solution(mesh):
    placed = (
        P(("dom", "rep"), None),
        P(),
        P(("dom", "rep"), None),
        P(("dom", "rep"), None, None, None),
        P(("dom", "rep")),
        P(("dom", "rep"), None, None),
        P(("dom", "rep"), None),
        P(("dom", "rep"), None),
    )
    return jax.shard_map(
        body,
        mesh=mesh,
        in_specs=placed,
        out_specs=(P(("dom", "rep"), None), P(("dom", "rep"), None), P()),
        check_vma=False,
    )
```
